512 devices in a mesh: pb: 64 (over z_lo, x, core), vert: 8 (over z_hi, y).
Axes of the slice: x: 4, y: 4, z: 16 (z_hi: 2, z_lo: 8; z = z_hi * 8 + z_lo), core: 2. Of those that a mesh axis runs over, the one named last changes fastest.
Arguments:
- cholesky: bfloat16 [64, 64, 1, 2, 128, 128], P('pb', None, None, None, 'vert'), may hold values from -6 to 6
- trial_rows: bfloat16 [64, 2, 32, 128], P('pb'), may hold values from -0.5 to 0.5
- occupied: int32 [64], replicated, may hold values from 16 to 32
- kpoint_map: int32 [64, 64], replicated, may hold values from 0 to 63, as said below
- partner: int32 [64], replicated, may hold values from 0 to 63, as said below
Outputs:
- paired_plus: bfloat16 [64, 64, 1, 2, 32, 128], P('pb', None, None, None, 'vert')
- paired_minus: bfloat16 [64, 64, 1, 2, 32, 128], P('pb', None, None, None, 'vert')
The draws below stay inside these ranges and needn't reach their ends.
Inputs may be any that keep to these rules, and one draw needn't show every extreme that they name: The k-points form a cyclic group of 64 elements labelled in an order drawn from the seed; kpoint_map[q, k] is the label of k - q, so kpoint_map[partner[q], kpoint_map[q, k]] = k. partner[q] is the label of -q in the same group; partner is an involution.
All inputs are finite; a program needn't handle non-finite values.
Results may differ from the reference program's by a relative error of at most 0.00165.
Values may be sent and summed in bfloat16 or wider, within the bound.
A program may use at most 64 MiB of HBM per device.

```python
import jax
import jax.numpy as jnp
from jax import lax

NORB = 128
NOCC = 32
CHOL = 1
NK = 64


def kpoint_labels(key):
    labels = jax.random.permutation(key, NK).astype(jnp.int32)
    element = jnp.argsort(labels).astype(jnp.int32)
    return (labels, element)


def draw_kpoint_map(key, part):
    labels, element = kpoint_labels(key)
    shifted = (element[None, :] - element[:, None]) % NK
    return labels[shifted].astype(jnp.int32)


def draw_partner(key, part):
    labels, element = kpoint_labels(key)
    return labels[(NK - element) % NK].astype(jnp.int32)


def draw_occupied(key, part):
    key = jax.random.fold_in(key, 7)
    key_one, key_two = jax.random.split(key)
    counts = jax.random.randint(key_one, (NK,), NOCC // 2, NOCC + 1).astype(jnp.int32)
    peak_at = jax.random.randint(key_two, (), 0, NK).astype(jnp.int32)
    counts = counts.at[peak_at].set(NOCC)
    counts = counts.at[(peak_at + 1) % NK].set(NOCC // 2)
    return counts.astype(jnp.int32)


def steps_of(rng, dims, pieces, smallest, largest):
    def one(dim, parts):
        steps = jax.random.uniform(jax.random.fold_in(jax.random.fold_in(rng, 6), dim), (parts,), jnp.float32, smallest / len(pieces), largest / len(pieces))
        return jnp.repeat(jnp.exp(steps), dims[dim] // parts).reshape((-1,) + (1,) * (len(dims) - dim - 1))

    factor_of = one(*pieces[0])
    for cut in pieces[1:]:
        factor_of = factor_of * one(*cut)
    return factor_of


def scatter_about(key, shape, deviation, limit, cuts=(), kind=jnp.bfloat16):
    gain = steps_of(key, shape, cuts, -0.22, 0.18) if cuts else 1.0
    result = jax.random.normal(key, shape, jnp.float32) * deviation * gain
    return jnp.minimum(jnp.maximum(result, -limit), limit).astype(kind)


def setup_inputs(seed: int = 0) -> dict:
    keys = jax.random.split(jax.random.key(seed), 6)
    return {
        "cholesky": scatter_about(keys[0], (NK, NK, CHOL, 2, NORB, NORB), 1.0, 6.0, ((0, 64), (4, 8))),
        "trial_rows": scatter_about(keys[1], (NK, 2, NOCC, NORB), NORB ** -0.5, 0.5, ((0, 64),)),
        "occupied": draw_occupied(jax.random.fold_in(keys[5], 71), 0),
        "kpoint_map": draw_kpoint_map(jax.random.fold_in(keys[5], 71), 0),
        "partner": draw_partner(jax.random.fold_in(keys[5], 71), 0),
    }


def rotate(orbitals, block, pattern, conjugate):
    trial_re = jnp.take(orbitals, 0, axis=-3)
    trial_im = jnp.take(orbitals, 1, axis=-3)
    block_re = block[:, :, 0]
    block_im = block[:, :, 1]

    def product(left, right):
        return jnp.einsum(pattern, left, right, precision=lax.Precision.HIGHEST, preferred_element_type=jnp.float32)

    if conjugate:
        real_part = product(trial_re, block_re) + product(trial_im, block_im)
        imag_part = product(trial_im, block_re) - product(trial_re, block_im)
    else:
        real_part = product(trial_re, block_re) - product(trial_im, block_im)
        imag_part = product(trial_re, block_im) + product(trial_im, block_re)
    return jnp.stack([real_part, imag_part], axis=2)


def combine(own_term, mirror_term):
    plus_part = ((own_term + mirror_term) * 0.5).astype(jnp.bfloat16)
    difference = own_term - mirror_term
    minus_part = (jnp.stack([difference[:, :, 1], -difference[:, :, 0]], axis=2) * 0.5).astype(jnp.bfloat16)
    return plus_part, minus_part


def reference(cholesky, trial_rows, occupied, kpoint_map, partner):
    live_rows = jnp.arange(NOCC, dtype=jnp.int32)[None, :] < occupied[:, None]
    masked = jnp.where(live_rows[:, None, :, None], trial_rows, jnp.zeros_like(trial_rows)).astype(jnp.float32)

    def per_transfer(qpoint):
        own_blk = cholesky[qpoint].astype(jnp.float32)
        mirror_blk = jnp.take(cholesky[partner[qpoint]], kpoint_map[qpoint], axis=0).astype(jnp.float32)
        own_term = rotate(masked, own_blk, "kar,kgsr->kgas", False)
        mirror_term = rotate(masked, mirror_blk, "kau,kgus->kgas", True)
        return combine(own_term, mirror_term)

    plus_all, minus_all = lax.map(per_transfer, jnp.arange(NK, dtype=jnp.int32))
    return jnp.transpose(plus_all, (1, 0, 2, 3, 4, 5)), jnp.transpose(minus_all, (1, 0, 2, 3, 4, 5))
```

```python
import functools

import jax
import jax.numpy as jnp
from jax import lax
from jax.experimental import pallas as pl
from jax.experimental.pallas import tpu as pltpu
from jax.sharding import PartitionSpec as P

MESH = pl.DeviceIdType.MESH
BITS = 19
TOP = 2**BITS - 1
BIAS = 128


def kpoint(jp, cp, y):
    return jp * 8 + ((y - jp + 8) % 4) * 2 + cp


def encode(own, real, imag):
    peak = jnp.maximum(jnp.maximum(jnp.abs(own), jnp.abs(real)), jnp.abs(imag))
    peak = jnp.max(peak, axis=0, keepdims=True)
    power = jnp.floor(jnp.log2(jnp.maximum(peak, 2.0**-100))) + 1.0
    scale = jnp.exp2(BITS - power)

    def code(value):
        return jnp.clip(jnp.round(value * scale), -TOP, TOP).astype(jnp.int32)

    biased = power.astype(jnp.int32) + BIAS
    row = lax.broadcasted_iota(jnp.int32, own.shape, 0) % 4
    part = jnp.where(row == 0, biased & 15, jnp.where(row == 1, biased >> 4, 0))
    mine = code(own)
    first = (code(real) << 12) | ((mine >> 8) & 4095)
    second = (code(imag) << 12) | ((mine & 255) << 4) | part
    return first, second


def unit_of(tile):
    part = tile & 15
    biased = part[4:5] + (part[5:6] << 4)
    return jnp.exp2((biased - (BIAS + BITS)).astype(jnp.float32))


def kernel(
    blocks_hbm, trial_ref, occupied, kpoint_map, partner, plus_ref, minus_ref,
    blocks, stage, work, masked, trials, outgoing, incoming,
    load_sem, block_send, block_recv, trial_send, trial_recv, term_send, term_recv,
):
    me, v = lax.axis_index("pb"), lax.axis_index("vert")
    zl, x, c = me // 8, (me // 2) % 4, me % 2
    zh, y = v // 4, v % 4
    z = zh * 8 + zl
    source_y = (x + zl) % 4
    mine = source_y == y
    trial_y = (x - z + 16) % 4
    trial_mine = mine & (trial_y == y)

    load = pltpu.make_async_copy(blocks_hbm, blocks, load_sem)
    load.start()

    barrier = pltpu.get_barrier_semaphore()

    def greet(pb, vert):
        pl.semaphore_signal(barrier, inc=1, device_id=(pb, vert), device_id_type=MESH)

    for d in range(1, 4):
        greet(me, zh * 4 + (y + d) % 4)

    def greet_terms(i, carry):
        for h in range(2):
            w = h * 4 + source_y

            @pl.when(jnp.logical_not((i == me) & (w == v)))
            def _():
                greet(i, w)

        return carry

    lax.fori_loop(0, 64, greet_terms, 0)

    def greet_trials(jp, carry):
        near = (z + (jp - z + 4 + 16) % 8 - 4 + 16) % 16
        w = (near // 8) * 4 + trial_y
        for cp in range(2):
            k = kpoint(jp, cp, y)

            @pl.when(jnp.logical_not((k == me) & (w == v)))
            def _():
                greet(k, w)

        return carry

    lax.fori_loop(0, 8, greet_trials, 0)

    live = lax.broadcasted_iota(jnp.int32, (32, 128), 0) < occupied[me]
    for part in range(2):
        value = trial_ref[part].astype(jnp.float32)
        masked[part] = jnp.where(live, value, 0.0).astype(jnp.bfloat16)

    away = pl.multiple_of((1 - zh) * 64, 64)

    def clear(jp, carry):
        for cp in range(2):
            for part in range(2):
                work[jp, cp, 1, part, pl.ds(away, 64), :] = jnp.zeros((64, 128), jnp.bfloat16)
        return carry

    lax.fori_loop(0, 8, clear, 0)
    load.wait()
    mirror_q = partner[me]

    def arrange(jp, carry):
        for to in range(4):
            for cp in range(2):
                k = kpoint(jp, cp, to)
                stage[to, jp, cp, 0, 0] = blocks[k, 0]
                stage[to, jp, cp, 0, 1] = -blocks[k, 1]
                stage[to, jp, cp, 1] = blocks[kpoint_map[mirror_q, k]]
        return carry

    lax.fori_loop(0, 8, arrange, 0)

    met = 147 - mine.astype(jnp.int32) - trial_mine.astype(jnp.int32)
    pl.semaphore_wait(barrier, met)

    def rows_from(jp, source):
        start = pl.multiple_of(zh * 64 + source * 16, 16)
        return work.at[jp, :, :, :, pl.ds(start, 16), :]

    def block_copy(i, d, source, target):
        jp = (zl + i) % 8
        return pltpu.make_async_remote_copy(
            src_ref=stage.at[target, jp],
            dst_ref=rows_from(jp, source),
            send_sem=block_send,
            recv_sem=block_recv.at[i, d],
            device_id=(me, zh * 4 + target),
            device_id_type=MESH,
        )

    def self_copy(i):
        jp = (zl + i) % 8
        return pltpu.make_async_copy(stage.at[y, jp], rows_from(jp, y), block_recv.at[i, 0])

    def trial_sends(i, carry):
        there = (z - ((i + 4) % 8 - 4) + 16) % 16
        x_to = (y + there) % 4
        w = (there // 8) * 4 + source_y
        slot = 2 * zl + c
        for cp in range(2):
            q = (there % 8) * 8 + x_to * 2 + cp
            own = (q == me) & (w == v)

            @pl.when(own)
            def _():
                pltpu.make_async_copy(masked, trials.at[slot], trial_recv.at[slot]).start()

            @pl.when(jnp.logical_not(own))
            def _():
                pltpu.make_async_remote_copy(
                    src_ref=masked,
                    dst_ref=trials.at[slot],
                    send_sem=trial_send,
                    recv_sem=trial_recv.at[slot],
                    device_id=(q, w),
                    device_id_type=MESH,
                ).start()

        return carry

    def block_sends(i, carry):
        self_copy(i).start()
        for d in range(1, 4):
            block_copy(i, d, y, (y + d) % 4).start()
        return carry

    block_sends(0, 0)
    lax.fori_loop(0, 8, trial_sends, 0)
    lax.fori_loop(1, 8, block_sends, 0)

    here = pl.multiple_of(zh * 64, 64)
    low = lax.broadcasted_iota(jnp.int32, (8, 128), 0) < 4

    def terms(i, carry):
        jp = (zl + i) % 8
        self_copy(i).wait()
        for d in range(1, 4):
            block_copy(i, d, (y - d + 4) % 4, y).wait_recv()
        for cp in range(2):
            slot = 2 * jp + cp
            pltpu.make_async_copy(masked, trials.at[slot], trial_recv.at[slot]).wait()
            real, imag = trials[slot, 0], trials[slot, 1]
            left = jnp.concatenate(
                [jnp.concatenate([real, imag], axis=1), jnp.concatenate([imag, -real], axis=1)], axis=0
            )
            mirror = jnp.dot(left, work[jp, cp, 1].reshape(256, 128), preferred_element_type=jnp.float32)
            right = jnp.concatenate(
                [work[jp, cp, 0, 0, pl.ds(here, 64), :], work[jp, cp, 0, 1, pl.ds(here, 64), :]], axis=1
            )
            own = lax.dot_general(
                left, right, (((1,), (1,)), ((), ())), preferred_element_type=jnp.float32
            )
            own = jnp.concatenate([own[:32], own[32:]], axis=1)
            first, second = encode(own, mirror[:32], mirror[32:])
            k = kpoint(jp, cp, y)
            for t in range(4):
                one, two = first[8 * t : 8 * t + 8], second[8 * t : 8 * t + 8]
                outgoing[slot, 2 * t] = jnp.where(low, one, pltpu.roll(two, 4, 0))
                outgoing[slot, 2 * t + 1] = jnp.where(low, pltpu.roll(one, 4, 0), two)
            for w in range(8):
                own_tile = (k == me) & (w == v)

                @pl.when(own_tile)
                def _():
                    pltpu.make_async_copy(outgoing.at[slot, w], incoming.at[zh, me], term_recv).start()

                @pl.when(jnp.logical_not(own_tile))
                def _():
                    pltpu.make_async_remote_copy(
                        src_ref=outgoing.at[slot, w],
                        dst_ref=incoming.at[zh, me],
                        send_sem=term_send,
                        recv_sem=term_recv,
                        device_id=(k, w),
                        device_id_type=MESH,
                    ).start()

        return carry

    lax.fori_loop(0, 8, terms, 0)

    pltpu.make_async_copy(incoming, incoming, term_recv).wait()

    lane = lax.broadcasted_iota(jnp.int32, (8, 128), 1) < 64
    stay = low == lane
    sign = jnp.where(low, 0.5, -0.5)

    def finish(q):
        far0, far1 = incoming[0, q], incoming[1, q]
        high = jnp.where(low, far0, pltpu.roll(far1, 4, 0)) & 4095
        rest = (jnp.where(low, pltpu.roll(far0, 4, 0), far1) >> 4) & 255
        code = ((high << 20) | (rest << 12)) >> 12
        own = code.astype(jnp.float32) * jnp.where(low, unit_of(far0), unit_of(far1))
        own = jnp.where(stay, own, pltpu.roll(pltpu.roll(own, 4, 0), 64, 1))
        p = partner[q]
        near0, near1 = incoming[0, p], incoming[1, p]
        mirror = (near0 >> 12).astype(jnp.float32) * unit_of(near0) + (near1 >> 12).astype(jnp.float32) * unit_of(near1)
        return (own + mirror) * 0.5, pltpu.roll(own - mirror, 4, 0) * sign

    def close(i, carry):
        results = [finish(2 * i), finish(2 * i + 1)]
        start = pl.multiple_of(i * 16, 16)
        plus_ref[pl.ds(start, 16), :] = jnp.concatenate([r[0] for r in results], axis=0).astype(jnp.bfloat16)
        minus_ref[pl.ds(start, 16), :] = jnp.concatenate([r[1] for r in results], axis=0).astype(jnp.bfloat16)
        return carry

    lax.fori_loop(0, 32, close, 0, unroll=2)

    pltpu.make_async_copy(stage.at[0:3], stage.at[0:3], block_send).wait()

    @pl.when(trial_mine)
    def _():
        pltpu.make_async_copy(trials.at[0:15], trials.at[0:15], trial_send).wait()

    @pl.when(jnp.logical_not(trial_mine))
    def _():
        pltpu.make_async_copy(trials, trials, trial_send).wait()

    @pl.when(mine)
    def _():
        pltpu.make_async_copy(outgoing.at[0:15], outgoing.at[0:15], term_send).wait()
        pltpu.make_async_copy(outgoing.at[0, 0:7], outgoing.at[0, 0:7], term_send).wait()

    @pl.when(jnp.logical_not(mine))
    def _():
        pltpu.make_async_copy(outgoing, outgoing, term_send).wait()


def local(cholesky, trial_rows, occupied, kpoint_map, partner):
    blocks = cholesky.reshape(64, 2, 16, 128)
    trial = trial_rows.reshape(2, 32, 128)
    vmem = pl.BlockSpec(memory_space=pltpu.VMEM)
    smem = pl.BlockSpec(memory_space=pltpu.SMEM)
    bf16, i32 = jnp.bfloat16, jnp.int32
    plus, minus = pl.pallas_call(
        kernel,
        out_shape=[jax.ShapeDtypeStruct((512, 128), bf16)] * 2,
        in_specs=[pl.BlockSpec(memory_space=pl.ANY), vmem, smem, smem, smem],
        out_specs=[vmem, vmem],
        scratch_shapes=[
            pltpu.VMEM((64, 2, 16, 128), bf16),
            pltpu.VMEM((4, 8, 2, 2, 2, 16, 128), bf16),
            pltpu.VMEM((8, 2, 2, 2, 128, 128), bf16),
            pltpu.VMEM((2, 32, 128), bf16),
            pltpu.VMEM((16, 2, 32, 128), bf16),
            pltpu.VMEM((16, 8, 8, 128), i32),
            pltpu.VMEM((2, 64, 8, 128), i32),
            pltpu.SemaphoreType.DMA,
            pltpu.SemaphoreType.DMA,
            pltpu.SemaphoreType.DMA((8, 4)),
            pltpu.SemaphoreType.DMA,
            pltpu.SemaphoreType.DMA((16,)),
            pltpu.SemaphoreType.DMA,
            pltpu.SemaphoreType.DMA,
        ],
        compiler_params=pltpu.CompilerParams(
            collective_id=0, has_side_effects=True, vmem_limit_bytes=32 * 2**20
        ),
    )(blocks, trial, occupied, kpoint_map, partner)
    shape = (1, 64, 1, 2, 4, 128)
    return plus.reshape(shape), minus.reshape(shape)


def solution(mesh):
    in_specs = (P("pb", None, None, None, "vert", None), P("pb", None, None, None), P(), P(), P())
    out_specs = (P("pb", None, None, None, "vert", None), P("pb", None, None, None, "vert", None))
    return jax.shard_map(local, mesh=mesh, in_specs=in_specs, out_specs=out_specs, check_vma=False)
```

```python
import functools

import jax
import jax.numpy as jnp
from jax import lax
from jax.experimental import pallas as pl
from jax.experimental.pallas import tpu as pltpu
from jax.sharding import PartitionSpec as P

MESH = pl.DeviceIdType.MESH
BITS = 19
TOP = 2**BITS - 1
BIAS = 128


def kpoint(jp, cp, y):
    return jp * 8 + ((y - jp + 8) % 4) * 2 + cp


def encode(own, real, imag):
    peak = jnp.maximum(jnp.maximum(jnp.abs(own), jnp.abs(real)), jnp.abs(imag))
    peak = jnp.max(peak, axis=0, keepdims=True)
    power = jnp.floor(jnp.log2(jnp.maximum(peak, 2.0**-100))) + 1.0
    scale = jnp.exp2(BITS - power)

    def code(value):
        return jnp.clip(jnp.round(value * scale), -TOP, TOP).astype(jnp.int32)

    biased = power.astype(jnp.int32) + BIAS
    row = lax.broadcasted_iota(jnp.int32, own.shape, 0) % 4
    part = jnp.where(row == 0, biased & 15, jnp.where(row == 1, biased >> 4, 0))
    mine = code(own)
    first = (code(real) << 12) | ((mine >> 8) & 4095)
    second = (code(imag) << 12) | ((mine & 255) << 4) | part
    return first, second


def unit_of(tile):
    part = tile & 15
    biased = part[4:5] + (part[5:6] << 4)
    return jnp.exp2((biased - (BIAS + BITS)).astype(jnp.float32))


def kernel(
    blocks_hbm, trial_hbm, occupied_hbm, map_hbm, partner_hbm, plus_ref, minus_ref,
    blocks, trial_ref, occupied, kpoint_map, partner, stage, work, trials, outgoing, incoming,
    load_sem, block_send, block_recv, trial_send, trial_recv, term_send, term_recv,
):
    me, v = lax.axis_index("pb"), lax.axis_index("vert")
    zl, x, c = me // 8, (me // 2) % 4, me % 2
    zh, y = v // 4, v % 4
    z = zh * 8 + zl
    source_y = (x + zl) % 4
    mine = source_y == y
    slot_me = 2 * zl + c
    first_zl = (zl + (y - x - zl + 12) % 4) % 8
    second_zl = (first_zl + 4) % 8

    def nearest(there):
        return (z + (there - z + 4 + 16) % 8 - 4 + 16) % 16

    barrier = pltpu.get_barrier_semaphore()

    def greet(pb, vert):
        pl.semaphore_signal(barrier, inc=1, device_id=(pb, vert), device_id_type=MESH)

    for d in range(1, 4):
        greet(me, zh * 4 + (y + d) % 4)

    def greet_terms(i, carry):
        for h in range(2):
            w = h * 4 + source_y

            @pl.when(jnp.logical_not((i == me) & (w == v)))
            def _():
                greet(i, w)

        return carry

    lax.fori_loop(0, 64, greet_terms, 0)

    for i in range(1, 8):
        greet(zl * 8 + ((x + i // 2) % 4) * 2 + (c + i) % 2, v)

    @pl.when(jnp.logical_not(mine))
    def _():
        near = nearest(first_zl)
        greet(first_zl * 8 + x * 2 + c, (near // 8) * 4 + y)

    near = nearest(second_zl)
    greet(second_zl * 8 + x * 2 + c, (near // 8) * 4 + y)

    loads = [
        pltpu.make_async_copy(a, b, load_sem.at[n])
        for n, (a, b) in enumerate(
            [(blocks_hbm, blocks), (trial_hbm, trial_ref), (occupied_hbm, occupied), (map_hbm, kpoint_map), (partner_hbm, partner)]
        )
    ]
    for load in loads:
        load.start()

    away = pl.multiple_of((1 - zh) * 64, 64)

    def clear(jp, carry):
        for cp in range(2):
            for part in range(2):
                work[jp, cp, 1, part, pl.ds(away, 64), :] = jnp.zeros((64, 128), jnp.bfloat16)
        return carry

    lax.fori_loop(0, 8, clear, 0)
    for load in loads:
        load.wait()

    @pl.when(mine)
    def _():
        live = lax.broadcasted_iota(jnp.int32, (32, 128), 0) < occupied[me]
        for part in range(2):
            value = trial_ref[part].astype(jnp.float32)
            trials[slot_me, part] = jnp.where(live, value, 0.0).astype(jnp.bfloat16)

    mirror_q = partner[me]

    def arrange(jp, carry):
        for to in range(4):
            for cp in range(2):
                k = kpoint(jp, cp, to)
                stage[to, jp, cp, 0, 0] = blocks[k, 0]
                stage[to, jp, cp, 0, 1] = -blocks[k, 1]
                stage[to, jp, cp, 1] = blocks[kpoint_map[mirror_q, k]]
        return carry

    lax.fori_loop(0, 8, arrange, 0)

    pl.semaphore_wait(barrier, 138 + 6 * mine.astype(jnp.int32))

    def rows_from(jp, source):
        start = pl.multiple_of(zh * 64 + source * 16, 16)
        return work.at[jp, :, :, :, pl.ds(start, 16), :]

    def block_copy(i, d, source, target):
        jp = (zl + i) % 8
        return pltpu.make_async_remote_copy(
            src_ref=stage.at[target, jp],
            dst_ref=rows_from(jp, source),
            send_sem=block_send,
            recv_sem=block_recv.at[i, d],
            device_id=(me, zh * 4 + target),
            device_id_type=MESH,
        )

    def self_copy(i):
        jp = (zl + i) % 8
        return pltpu.make_async_copy(stage.at[y, jp], rows_from(jp, y), block_recv.at[i, 0])

    def trial_copy(slot, pb, vert):
        return pltpu.make_async_remote_copy(
            src_ref=trials.at[slot],
            dst_ref=trials.at[slot],
            send_sem=trial_send,
            recv_sem=trial_recv.at[slot],
            device_id=(pb, vert),
            device_id_type=MESH,
        )

    def forward(there):
        for i in range(1, 8):
            trial_copy(2 * there + c, zl * 8 + ((x + i // 2) % 4) * 2 + (c + i) % 2, v).start()

    def block_sends(i, carry):
        self_copy(i).start()
        for d in range(1, 4):
            block_copy(i, d, y, (y + d) % 4).start()
        return carry

    @pl.when(mine)
    def _():
        forward(zl)
        for d in (1, -1, 2, -2, 3, -3, -4):
            there = (z - d + 16) % 16
            trial_copy(slot_me, (there % 8) * 8 + x * 2 + c, (there // 8) * 4 + y).start()

    block_sends(0, 0)
    block_sends(1, 0)

    @pl.when(jnp.logical_not(mine))
    def _():
        trial_copy(2 * first_zl + c, me, v).wait_recv()
        forward(first_zl)


    here = pl.multiple_of(zh * 64, 64)
    low = lax.broadcasted_iota(jnp.int32, (8, 128), 0) < 4

    def terms(i, carry):
        jp = (zl + i) % 8

        @pl.when(i < 6)
        def _():
            block_sends(i + 2, 0)

        @pl.when(i == 1)
        def _():
            trial_copy(2 * second_zl + c, me, v).wait_recv()
            forward(second_zl)

        self_copy(i).wait()
        for d in range(1, 4):
            block_copy(i, d, (y - d + 4) % 4, y).wait_recv()
        for cp in range(2):
            slot = 2 * jp + cp

            @pl.when((cp != c) | ((jp != first_zl) & (jp != second_zl)))
            def _():
                trial_copy(slot, me, v).wait_recv()

            real, imag = trials[slot, 0], trials[slot, 1]
            left = jnp.concatenate(
                [jnp.concatenate([real, imag], axis=1), jnp.concatenate([imag, -real], axis=1)], axis=0
            )
            mirror = jnp.dot(left, work[jp, cp, 1].reshape(256, 128), preferred_element_type=jnp.float32)
            right = jnp.concatenate(
                [work[jp, cp, 0, 0, pl.ds(here, 64), :], work[jp, cp, 0, 1, pl.ds(here, 64), :]], axis=1
            )
            own = lax.dot_general(
                left, right, (((1,), (1,)), ((), ())), preferred_element_type=jnp.float32
            )
            own = jnp.concatenate([own[:32], own[32:]], axis=1)
            first, second = encode(own, mirror[:32], mirror[32:])
            k = kpoint(jp, cp, y)
            for t in range(4):
                one, two = first[8 * t : 8 * t + 8], second[8 * t : 8 * t + 8]
                outgoing[slot, 2 * t] = jnp.where(low, one, pltpu.roll(two, 4, 0))
                outgoing[slot, 2 * t + 1] = jnp.where(low, pltpu.roll(one, 4, 0), two)
            for w in range(8):
                own_tile = (k == me) & (w == v)

                @pl.when(own_tile)
                def _():
                    pltpu.make_async_copy(outgoing.at[slot, w], incoming.at[zh, me], term_recv).start()

                @pl.when(jnp.logical_not(own_tile))
                def _():
                    pltpu.make_async_remote_copy(
                        src_ref=outgoing.at[slot, w],
                        dst_ref=incoming.at[zh, me],
                        send_sem=term_send,
                        recv_sem=term_recv,
                        device_id=(k, w),
                        device_id_type=MESH,
                    ).start()

        return carry

    lax.fori_loop(0, 8, terms, 0)

    pltpu.make_async_copy(incoming, incoming, term_recv).wait()

    lane = lax.broadcasted_iota(jnp.int32, (8, 128), 1) < 64
    stay = low == lane
    sign = jnp.where(low, 0.5, -0.5)

    def finish(q):
        far0, far1 = incoming[0, q], incoming[1, q]
        high = jnp.where(low, far0, pltpu.roll(far1, 4, 0)) & 4095
        rest = (jnp.where(low, pltpu.roll(far0, 4, 0), far1) >> 4) & 255
        code = ((high << 20) | (rest << 12)) >> 12
        own = code.astype(jnp.float32) * jnp.where(low, unit_of(far0), unit_of(far1))
        own = jnp.where(stay, own, pltpu.roll(pltpu.roll(own, 4, 0), 64, 1))
        p = partner[q]
        near0, near1 = incoming[0, p], incoming[1, p]
        mirror = (near0 >> 12).astype(jnp.float32) * unit_of(near0) + (near1 >> 12).astype(jnp.float32) * unit_of(near1)
        return (own + mirror) * 0.5, pltpu.roll(own - mirror, 4, 0) * sign

    def close(i, carry):
        results = [finish(2 * i), finish(2 * i + 1)]
        start = pl.multiple_of(i * 16, 16)
        plus_ref[pl.ds(start, 16), :] = jnp.concatenate([r[0] for r in results], axis=0).astype(jnp.bfloat16)
        minus_ref[pl.ds(start, 16), :] = jnp.concatenate([r[1] for r in results], axis=0).astype(jnp.bfloat16)
        return carry

    lax.fori_loop(0, 32, close, 0, unroll=2)

    pltpu.make_async_copy(stage.at[0:3], stage.at[0:3], block_send).wait()

    pltpu.make_async_copy(trials.at[0:14], trials.at[0:14], trial_send).wait()

    @pl.when(mine)
    def _():
        pltpu.make_async_copy(trials.at[0:7], trials.at[0:7], trial_send).wait()

    @pl.when(mine)
    def _():
        pltpu.make_async_copy(outgoing.at[0:15], outgoing.at[0:15], term_send).wait()
        pltpu.make_async_copy(outgoing.at[0, 0:7], outgoing.at[0, 0:7], term_send).wait()

    @pl.when(jnp.logical_not(mine))
    def _():
        pltpu.make_async_copy(outgoing, outgoing, term_send).wait()


def local(cholesky, trial_rows, occupied, kpoint_map, partner):
    blocks = cholesky.reshape(64, 2, 16, 128)
    trial = trial_rows.reshape(2, 32, 128)
    vmem = pl.BlockSpec(memory_space=pltpu.VMEM)
    bf16, i32 = jnp.bfloat16, jnp.int32
    plus, minus = pl.pallas_call(
        kernel,
        out_shape=[jax.ShapeDtypeStruct((512, 128), bf16)] * 2,
        in_specs=[pl.BlockSpec(memory_space=pl.ANY)] * 5,
        out_specs=[vmem, vmem],
        scratch_shapes=[
            pltpu.VMEM((64, 2, 16, 128), bf16),
            pltpu.VMEM((2, 32, 128), bf16),
            pltpu.SMEM((64,), i32),
            pltpu.SMEM((64, 64), i32),
            pltpu.SMEM((64,), i32),
            pltpu.VMEM((4, 8, 2, 2, 2, 16, 128), bf16),
            pltpu.VMEM((8, 2, 2, 2, 128, 128), bf16),
            pltpu.VMEM((16, 2, 32, 128), bf16),
            pltpu.VMEM((16, 8, 8, 128), i32),
            pltpu.VMEM((2, 64, 8, 128), i32),
            pltpu.SemaphoreType.DMA((5,)),
            pltpu.SemaphoreType.DMA,
            pltpu.SemaphoreType.DMA((8, 4)),
            pltpu.SemaphoreType.DMA,
            pltpu.SemaphoreType.DMA((16,)),
            pltpu.SemaphoreType.DMA,
            pltpu.SemaphoreType.DMA,
        ],
        compiler_params=pltpu.CompilerParams(
            collective_id=0, has_side_effects=True, vmem_limit_bytes=60 * 2**20
        ),
    )(blocks, trial, occupied, kpoint_map, partner)
    shape = (1, 64, 1, 2, 4, 128)
    return plus.reshape(shape), minus.reshape(shape)


def solution(mesh):
    in_specs = (P("pb", None, None, None, "vert", None), P("pb", None, None, None), P(), P(), P())
    out_specs = (P("pb", None, None, None, "vert", None), P("pb", None, None, None, "vert", None))
    return jax.shard_map(local, mesh=mesh, in_specs=in_specs, out_specs=out_specs, check_vma=False)
```

```python
import functools

import jax
import jax.numpy as jnp
from jax import lax
from jax.experimental import pallas as pl
from jax.experimental.pallas import tpu as pltpu
from jax.sharding import PartitionSpec as P

MESH = pl.DeviceIdType.MESH
BITS = 17
TOP = 2**BITS - 1
BIAS = 128


def kpoint(jp, cp, y):
    return jp * 8 + ((y - jp + 8) % 4) * 2 + cp


def encode(own, real, imag):
    peak = jnp.maximum(jnp.maximum(jnp.abs(own), jnp.abs(real)), jnp.abs(imag))
    peak = jnp.max(peak, axis=0, keepdims=True)
    power = jnp.floor(jnp.log2(jnp.maximum(peak, 2.0**-100))) + 1.0
    scale = jnp.exp2(BITS - power)
    biased = (power.astype(jnp.int32) + BIAS) << 24
    row = lax.broadcasted_iota(jnp.int32, (8, 128), 0)
    low = row < 4
    place = (row % 4) * 6

    def code(value, t):
        return jnp.clip(jnp.round(value[8 * t : 8 * t + 8] * scale), -TOP, TOP).astype(jnp.int32)

    messages = []
    for t in range(4):
        a, b, c = code(real, t), code(imag, t), code(own, t)
        mirror = ((a >> 2) << 16) | ((b >> 2) & 65535)
        pairs = ((c >> 2) << 16) | pltpu.roll((c >> 2) & 65535, 6, 0)
        small = (((a & 3) << 4) | ((b & 3) << 2) | (c & 3)) << place
        small = small + pltpu.roll(small, 7, 0)
        small = (small + pltpu.roll(small, 6, 0)) | biased
        rest = jnp.where(row % 4 < 2, pairs, pltpu.roll(small, 2, 0))
        messages.append(jnp.where(low, mirror, pltpu.roll(rest, 4, 0)))
        messages.append(jnp.where(low, pltpu.roll(mirror, 4, 0), rest))
    return messages


def unit_of(word):
    return jnp.exp2((((word >> 24) & 255) - (BIAS + BITS)).astype(jnp.float32))


def kernel(
    blocks_hbm, trial_hbm, occupied_hbm, map_hbm, partner_hbm, plus_ref, minus_ref,
    blocks, trial_ref, occupied, kpoint_map, partner, stage, work, trials, outgoing, incoming,
    load_sem, block_send, block_recv, trial_send, trial_recv, term_send, term_recv,
):
    me, v = lax.axis_index("pb"), lax.axis_index("vert")
    zl, x, c = me // 8, (me // 2) % 4, me % 2
    zh, y = v // 4, v % 4
    z = zh * 8 + zl
    source_y = (x + zl) % 4
    mine = source_y == y
    slot_me = 2 * zl + c
    first_zl = (zl + (y - x - zl + 12) % 4) % 8
    second_zl = (first_zl + 4) % 8

    def nearest(there):
        return (z + (there - z + 4 + 16) % 8 - 4 + 16) % 16

    barrier = pltpu.get_barrier_semaphore()

    def greet(pb, vert):
        pl.semaphore_signal(barrier, inc=1, device_id=(pb, vert), device_id_type=MESH)

    for d in range(1, 4):
        greet(me, zh * 4 + (y + d) % 4)

    def greet_terms(i, carry):
        for h in range(2):
            w = h * 4 + source_y

            @pl.when(jnp.logical_not((i == me) & (w == v)))
            def _():
                greet(i, w)

        return carry

    lax.fori_loop(0, 64, greet_terms, 0)

    for i in range(1, 8):
        greet(zl * 8 + ((x + i // 2) % 4) * 2 + (c + i) % 2, v)

    @pl.when(jnp.logical_not(mine))
    def _():
        near = nearest(first_zl)
        greet(first_zl * 8 + x * 2 + c, (near // 8) * 4 + y)

    near = nearest(second_zl)
    greet(second_zl * 8 + x * 2 + c, (near // 8) * 4 + y)

    loads = [
        pltpu.make_async_copy(a, b, load_sem.at[n])
        for n, (a, b) in enumerate(
            [(blocks_hbm, blocks), (trial_hbm, trial_ref), (occupied_hbm, occupied), (map_hbm, kpoint_map), (partner_hbm, partner)]
        )
    ]
    for load in loads:
        load.start()

    away = pl.multiple_of((1 - zh) * 64, 64)

    def clear(jp, carry):
        for cp in range(2):
            for part in range(2):
                work[jp, cp, 1, part, pl.ds(away, 64), :] = jnp.zeros((64, 128), jnp.bfloat16)
        return carry

    lax.fori_loop(0, 8, clear, 0)
    for load in loads:
        load.wait()

    @pl.when(mine)
    def _():
        live = lax.broadcasted_iota(jnp.int32, (32, 128), 0) < occupied[me]
        for part in range(2):
            value = trial_ref[part].astype(jnp.float32)
            trials[slot_me, part] = jnp.where(live, value, 0.0).astype(jnp.bfloat16)

    mirror_q = partner[me]

    def arrange(jp, carry):
        for to in range(4):
            for cp in range(2):
                k = kpoint(jp, cp, to)
                stage[to, jp, cp, 0, 0] = blocks[k, 0]
                stage[to, jp, cp, 0, 1] = -blocks[k, 1]
                stage[to, jp, cp, 1] = blocks[kpoint_map[mirror_q, k]]
        return carry

    lax.fori_loop(0, 8, arrange, 0)

    pl.semaphore_wait(barrier, 138 + 6 * mine.astype(jnp.int32))

    def rows_from(jp, source):
        start = pl.multiple_of(zh * 64 + source * 16, 16)
        return work.at[jp, :, :, :, pl.ds(start, 16), :]

    def block_copy(i, d, source, target):
        jp = (zl + i) % 8
        return pltpu.make_async_remote_copy(
            src_ref=stage.at[target, jp],
            dst_ref=rows_from(jp, source),
            send_sem=block_send,
            recv_sem=block_recv.at[i, d],
            device_id=(me, zh * 4 + target),
            device_id_type=MESH,
        )

    def self_copy(i):
        jp = (zl + i) % 8
        return pltpu.make_async_copy(stage.at[y, jp], rows_from(jp, y), block_recv.at[i, 0])

    def trial_copy(slot, pb, vert):
        return pltpu.make_async_remote_copy(
            src_ref=trials.at[slot],
            dst_ref=trials.at[slot],
            send_sem=trial_send,
            recv_sem=trial_recv.at[slot],
            device_id=(pb, vert),
            device_id_type=MESH,
        )

    def forward(there):
        for i in range(1, 8):
            trial_copy(2 * there + c, zl * 8 + ((x + i // 2) % 4) * 2 + (c + i) % 2, v).start()

    def block_sends(i, carry):
        self_copy(i).start()
        for d in range(1, 4):
            block_copy(i, d, y, (y + d) % 4).start()
        return carry

    block_sends(0, 0)

    @pl.when(mine)
    def _():
        forward(zl)
        for d in (1, -1, 2, -2, 3, -3, -4):
            there = (z - d + 16) % 16
            trial_copy(slot_me, (there % 8) * 8 + x * 2 + c, (there // 8) * 4 + y).start()

    block_sends(1, 0)

    @pl.when(jnp.logical_not(mine))
    def _():
        trial_copy(2 * first_zl + c, me, v).wait_recv()
        forward(first_zl)


    here = pl.multiple_of(zh * 64, 64)
    low = lax.broadcasted_iota(jnp.int32, (8, 128), 0) < 4

    def terms(i, carry):
        jp = (zl + i) % 8

        @pl.when(i < 6)
        def _():
            block_sends(i + 2, 0)

        @pl.when(i == 1)
        def _():
            trial_copy(2 * second_zl + c, me, v).wait_recv()
            forward(second_zl)

        self_copy(i).wait()
        for d in range(1, 4):
            block_copy(i, d, (y - d + 4) % 4, y).wait_recv()
        for cp in range(2):
            slot = 2 * jp + cp

            @pl.when((cp != c) | ((jp != first_zl) & (jp != second_zl)))
            def _():
                trial_copy(slot, me, v).wait_recv()

            real, imag = trials[slot, 0], trials[slot, 1]
            left = jnp.concatenate(
                [jnp.concatenate([real, imag], axis=1), jnp.concatenate([imag, -real], axis=1)], axis=0
            )
            mirror = jnp.dot(left, work[jp, cp, 1].reshape(256, 128), preferred_element_type=jnp.float32)
            right = jnp.concatenate(
                [work[jp, cp, 0, 0, pl.ds(here, 64), :], work[jp, cp, 0, 1, pl.ds(here, 64), :]], axis=1
            )
            own = lax.dot_general(
                left, right, (((1,), (1,)), ((), ())), preferred_element_type=jnp.float32
            )
            own = jnp.concatenate([own[:32], own[32:]], axis=1)
            messages = encode(own, mirror[:32], mirror[32:])
            k = kpoint(jp, cp, y)
            for w in range(8):
                outgoing[slot, w] = messages[w][:7]
            for w in range(8):
                own_tile = (k == me) & (w == v)

                @pl.when(own_tile)
                def _():
                    pltpu.make_async_copy(outgoing.at[slot, w], incoming.at[zh, me], term_recv).start()

                @pl.when(jnp.logical_not(own_tile))
                def _():
                    pltpu.make_async_remote_copy(
                        src_ref=outgoing.at[slot, w],
                        dst_ref=incoming.at[zh, me],
                        send_sem=term_send,
                        recv_sem=term_recv,
                        device_id=(k, w),
                        device_id_type=MESH,
                    ).start()

        return carry

    lax.fori_loop(0, 8, terms, 0)

    pltpu.make_async_copy(incoming, incoming, term_recv).wait()

    lane = lax.broadcasted_iota(jnp.int32, (8, 128), 1) < 64
    stay = low == lane
    sign = jnp.where(low, 0.5, -0.5)

    row = lax.broadcasted_iota(jnp.int32, (8, 128), 0)
    own_place = (row % 4) * 6
    mirror_place = own_place + jnp.where(low, 4, 2)

    def own_of(q):
        parts = []
        for h in range(2):
            pairs = incoming[h, q, pl.ds(4, 2)]
            parts += [pairs >> 16, (pairs << 16) >> 16]
        first, second = incoming[0, q, pl.ds(6, 1)], incoming[1, q, pl.ds(6, 1)]
        small = (jnp.where(low, first, second) >> own_place) & 3
        code = (jnp.concatenate(parts, axis=0) << 2) | small
        own = code.astype(jnp.float32) * jnp.where(low, unit_of(first), unit_of(second))
        return jnp.where(stay, own, pltpu.roll(pltpu.roll(own, 4, 0), 64, 1))

    def mirror_of(p, h):
        words, last = incoming[h, p, pl.ds(0, 4)], incoming[h, p, pl.ds(6, 1)]
        code = jnp.concatenate([words >> 16, (words << 16) >> 16], axis=0)
        code = (code << 2) | ((last >> mirror_place) & 3)
        return code.astype(jnp.float32) * unit_of(last)

    def finish(q):
        own = own_of(q)
        p = partner[q]
        mirror = mirror_of(p, 0) + mirror_of(p, 1)
        return (own + mirror) * 0.5, pltpu.roll(own - mirror, 4, 0) * sign

    def close(i, carry):
        results = [finish(2 * i), finish(2 * i + 1)]
        start = pl.multiple_of(i * 16, 16)
        plus_ref[pl.ds(start, 16), :] = jnp.concatenate([r[0] for r in results], axis=0).astype(jnp.bfloat16)
        minus_ref[pl.ds(start, 16), :] = jnp.concatenate([r[1] for r in results], axis=0).astype(jnp.bfloat16)
        return carry

    lax.fori_loop(0, 32, close, 0, unroll=2)

    pltpu.make_async_copy(stage.at[0:3], stage.at[0:3], block_send).wait()

    pltpu.make_async_copy(trials.at[0:14], trials.at[0:14], trial_send).wait()

    @pl.when(mine)
    def _():
        pltpu.make_async_copy(trials.at[0:7], trials.at[0:7], trial_send).wait()

    @pl.when(mine)
    def _():
        pltpu.make_async_copy(outgoing.at[0:15], outgoing.at[0:15], term_send).wait()
        pltpu.make_async_copy(outgoing.at[0, 0:7], outgoing.at[0, 0:7], term_send).wait()

    @pl.when(jnp.logical_not(mine))
    def _():
        pltpu.make_async_copy(outgoing, outgoing, term_send).wait()


def local(cholesky, trial_rows, occupied, kpoint_map, partner):
    blocks = cholesky.reshape(64, 2, 16, 128)
    trial = trial_rows.reshape(2, 32, 128)
    vmem = pl.BlockSpec(memory_space=pltpu.VMEM)
    bf16, i32 = jnp.bfloat16, jnp.int32
    plus, minus = pl.pallas_call(
        kernel,
        out_shape=[jax.ShapeDtypeStruct((512, 128), bf16)] * 2,
        in_specs=[pl.BlockSpec(memory_space=pl.ANY)] * 5,
        out_specs=[vmem, vmem],
        scratch_shapes=[
            pltpu.VMEM((64, 2, 16, 128), bf16),
            pltpu.VMEM((2, 32, 128), bf16),
            pltpu.SMEM((64,), i32),
            pltpu.SMEM((64, 64), i32),
            pltpu.SMEM((64,), i32),
            pltpu.VMEM((4, 8, 2, 2, 2, 16, 128), bf16),
            pltpu.VMEM((8, 2, 2, 2, 128, 128), bf16),
            pltpu.VMEM((16, 2, 32, 128), bf16),
            pltpu.VMEM((16, 8, 7, 128), i32),
            pltpu.VMEM((2, 64, 7, 128), i32),
            pltpu.SemaphoreType.DMA((5,)),
            pltpu.SemaphoreType.DMA,
            pltpu.SemaphoreType.DMA((8, 4)),
            pltpu.SemaphoreType.DMA,
            pltpu.SemaphoreType.DMA((16,)),
            pltpu.SemaphoreType.DMA,
            pltpu.SemaphoreType.DMA,
        ],
        compiler_params=pltpu.CompilerParams(
            collective_id=0, has_side_effects=True, vmem_limit_bytes=60 * 2**20
        ),
    )(blocks, trial, occupied, kpoint_map, partner)
    shape = (1, 64, 1, 2, 4, 128)
    return plus.reshape(shape), minus.reshape(shape)


def solution(mesh):
    in_specs = (P("pb", None, None, None, "vert", None), P("pb", None, None, None), P(), P(), P())
    out_specs = (P("pb", None, None, None, "vert", None), P("pb", None, None, None, "vert", None))
    return jax.shard_map(local, mesh=mesh, in_specs=in_specs, out_specs=out_specs, check_vma=False)
```

```python
import functools

import jax
import jax.numpy as jnp
from jax import lax
from jax.experimental import pallas as pl
from jax.experimental.pallas import tpu as pltpu
from jax.sharding import PartitionSpec as P

MESH = pl.DeviceIdType.MESH
BITS = 17
TOP = 2**BITS - 1
BIAS = 128


def kpoint(jp, cp, y, zl):
    return jp * 8 + ((y - jp + zl + 8) % 4) * 2 + cp


def encode(own, real, imag):
    peak = jnp.maximum(jnp.maximum(jnp.abs(own), jnp.abs(real)), jnp.abs(imag))
    peak = jnp.max(peak, axis=0, keepdims=True)
    power = jnp.floor(jnp.log2(jnp.maximum(peak, 2.0**-100))) + 1.0
    scale = jnp.exp2(BITS - power)
    biased = (power.astype(jnp.int32) + BIAS) << 24
    row = lax.broadcasted_iota(jnp.int32, (8, 128), 0)
    low = row < 4
    place = (row % 4) * 6

    def code(value, t):
        return jnp.clip(jnp.round(value[8 * t : 8 * t + 8] * scale), -TOP, TOP).astype(jnp.int32)

    messages = []
    for t in range(4):
        a, b, c = code(real, t), code(imag, t), code(own, t)
        mirror = ((a >> 2) << 16) | ((b >> 2) & 65535)
        pairs = ((c >> 2) << 16) | pltpu.roll((c >> 2) & 65535, 6, 0)
        small = (((a & 3) << 4) | ((b & 3) << 2) | (c & 3)) << place
        small = small + pltpu.roll(small, 7, 0)
        small = (small + pltpu.roll(small, 6, 0)) | biased
        rest = jnp.where(row % 4 < 2, pairs, pltpu.roll(small, 2, 0))
        messages.append(jnp.where(low, mirror, pltpu.roll(rest, 4, 0)))
        messages.append(jnp.where(low, pltpu.roll(mirror, 4, 0), rest))
    return messages


def unit_of(word):
    return jnp.exp2((((word >> 24) & 255) - (BIAS + BITS)).astype(jnp.float32))


def kernel(
    blocks_hbm, trial_hbm, occupied_hbm, map_hbm, partner_hbm, plus_ref, minus_ref,
    blocks, trial_ref, masked, occupied, kpoint_map, partner, stage, work, trials, outgoing, incoming,
    load_sem, block_send, block_recv, trial_send, trial_recv, term_send, term_recv,
):
    me, v = lax.axis_index("pb"), lax.axis_index("vert")
    zl, x, c = me // 8, (me // 2) % 4, me % 2
    zh, y = v // 4, v % 4
    z = zh * 8 + zl
    mine = x == y
    slot_me = 2 * zl + c
    first_zl = (zl + (y - x + 4) % 4) % 8
    second_zl = (first_zl + 4) % 8

    def nearest(there):
        return (z + (there - z + 4 + 16) % 8 - 4 + 16) % 16

    barrier = pltpu.get_barrier_semaphore()

    def greet(pb, vert):
        pl.semaphore_signal(barrier, inc=1, device_id=(pb, vert), device_id_type=MESH)

    for d in range(1, 4):
        greet(me, zh * 4 + (y + d) % 4)

    def greet_terms(i, carry):
        for h in range(2):
            w = h * 4 + (x + zl - i // 8 + 8) % 4

            @pl.when(jnp.logical_not((i == me) & (w == v)))
            def _():
                greet(i, w)

        return carry

    lax.fori_loop(0, 64, greet_terms, 0)

    for i in range(1, 8):
        greet(zl * 8 + ((x + i // 2) % 4) * 2 + (c + i) % 2, v)

    @pl.when(jnp.logical_not(mine))
    def _():
        near = nearest(first_zl)
        greet(first_zl * 8 + x * 2 + c, (near // 8) * 4 + y)

    near = nearest(second_zl)
    greet(second_zl * 8 + x * 2 + c, (near // 8) * 4 + y)

    loads = [
        pltpu.make_async_copy(a, b, load_sem.at[n])
        for n, (a, b) in enumerate(
            [(blocks_hbm, blocks), (trial_hbm, trial_ref), (occupied_hbm, occupied), (map_hbm, kpoint_map), (partner_hbm, partner)]
        )
    ]
    for load in loads:
        load.start()

    away = pl.multiple_of((1 - zh) * 64, 64)

    def clear(jp, carry):
        for cp in range(2):
            for part in range(2):
                work[jp, cp, 1, part, pl.ds(away, 64), :] = jnp.zeros((64, 128), jnp.bfloat16)
        return carry

    lax.fori_loop(0, 8, clear, 0)
    for load in loads:
        load.wait()

    live = lax.broadcasted_iota(jnp.int32, (32, 128), 0) < occupied[me]
    for part in range(2):
        value = trial_ref[part].astype(jnp.float32)
        masked[part] = jnp.where(live, value, 0.0).astype(jnp.bfloat16)

    @pl.when(mine)
    def _():
        trials[slot_me] = masked[...]

    mirror_q = partner[me]

    def arrange(jp, carry):
        for to in range(4):
            for cp in range(2):
                k = kpoint(jp, cp, to, zl)
                stage[to, jp, cp, 0, 0] = blocks[k, 0]
                stage[to, jp, cp, 0, 1] = -blocks[k, 1]
                stage[to, jp, cp, 1] = blocks[kpoint_map[mirror_q, k]]
        return carry

    lax.fori_loop(0, 8, arrange, 0)

    pl.semaphore_wait(barrier, 140 - 2 * mine.astype(jnp.int32))

    def rows_from(jp, source):
        start = pl.multiple_of(zh * 64 + source * 16, 16)
        return work.at[jp, :, :, :, pl.ds(start, 16), :]

    def block_copy(i, d, source, target):
        jp = (zl + i) % 8
        return pltpu.make_async_remote_copy(
            src_ref=stage.at[target, jp],
            dst_ref=rows_from(jp, source),
            send_sem=block_send,
            recv_sem=block_recv.at[i, d],
            device_id=(me, zh * 4 + target),
            device_id_type=MESH,
        )

    def self_copy(i):
        jp = (zl + i) % 8
        return pltpu.make_async_copy(stage.at[y, jp], rows_from(jp, y), block_recv.at[i, 0])

    def trial_copy(slot, pb, vert, source=None):
        return pltpu.make_async_remote_copy(
            src_ref=trials.at[slot] if source is None else source,
            dst_ref=trials.at[slot],
            send_sem=trial_send,
            recv_sem=trial_recv.at[slot],
            device_id=(pb, vert),
            device_id_type=MESH,
        )

    def forward(there):
        for i in range(1, 8):
            trial_copy(2 * there + c, zl * 8 + ((x + i // 2) % 4) * 2 + (c + i) % 2, v).start()

    def block_sends(i, carry):
        self_copy(i).start()
        for d in range(1, 4):
            block_copy(i, d, y, (y + d) % 4).start()
        return carry

    block_sends(0, 0)

    def trial_along(d):
        there = (z - d + 16) % 16
        trial_copy(slot_me, (there % 8) * 8 + x * 2 + c, (there // 8) * 4 + y, masked).start()

    offset = (y - x + 4) % 4

    @pl.when(mine)
    def _():
        forward(zl)

    @pl.when(jnp.logical_not(mine))
    def _():
        trial_along(offset)

    trial_along(offset - 4)
    block_sends(1, 0)

    @pl.when(jnp.logical_not(mine))
    def _():
        trial_copy(2 * first_zl + c, me, v).wait_recv()
        forward(first_zl)


    here = pl.multiple_of(zh * 64, 64)
    low = lax.broadcasted_iota(jnp.int32, (8, 128), 0) < 4

    def terms(i, carry):
        jp = (zl + i) % 8

        @pl.when(i < 6)
        def _():
            block_sends(i + 2, 0)

        @pl.when(i == 1)
        def _():
            trial_copy(2 * second_zl + c, me, v).wait_recv()
            forward(second_zl)

        self_copy(i).wait()
        for d in range(1, 4):
            block_copy(i, d, (y - d + 4) % 4, y).wait_recv()
        for cp in range(2):
            slot = 2 * jp + cp

            @pl.when((cp != c) | ((jp != first_zl) & (jp != second_zl)))
            def _():
                trial_copy(slot, me, v).wait_recv()

            real, imag = trials[slot, 0], trials[slot, 1]
            left = jnp.concatenate(
                [jnp.concatenate([real, imag], axis=1), jnp.concatenate([imag, -real], axis=1)], axis=0
            )
            mirror = jnp.dot(left, work[jp, cp, 1].reshape(256, 128), preferred_element_type=jnp.float32)
            right = jnp.concatenate(
                [work[jp, cp, 0, 0, pl.ds(here, 64), :], work[jp, cp, 0, 1, pl.ds(here, 64), :]], axis=1
            )
            own = lax.dot_general(
                left, right, (((1,), (1,)), ((), ())), preferred_element_type=jnp.float32
            )
            own = jnp.concatenate([own[:32], own[32:]], axis=1)
            messages = encode(own, mirror[:32], mirror[32:])
            k = kpoint(jp, cp, y, zl)
            for w in range(8):
                outgoing[slot, w] = messages[w][:7]
            for w in range(8):
                own_tile = (k == me) & (w == v)

                @pl.when(own_tile)
                def _():
                    pltpu.make_async_copy(outgoing.at[slot, w], incoming.at[zh, me], term_recv).start()

                @pl.when(jnp.logical_not(own_tile))
                def _():
                    pltpu.make_async_remote_copy(
                        src_ref=outgoing.at[slot, w],
                        dst_ref=incoming.at[zh, me],
                        send_sem=term_send,
                        recv_sem=term_recv,
                        device_id=(k, w),
                        device_id_type=MESH,
                    ).start()

        return carry

    lax.fori_loop(0, 8, terms, 0)

    pltpu.make_async_copy(incoming, incoming, term_recv).wait()

    lane = lax.broadcasted_iota(jnp.int32, (8, 128), 1) < 64
    stay = low == lane
    sign = jnp.where(low, 0.5, -0.5)

    row = lax.broadcasted_iota(jnp.int32, (8, 128), 0)
    own_place = (row % 4) * 6
    mirror_place = own_place + jnp.where(low, 4, 2)

    def own_of(q):
        parts = []
        for h in range(2):
            pairs = incoming[h, q, pl.ds(4, 2)]
            parts += [pairs >> 16, (pairs << 16) >> 16]
        first, second = incoming[0, q, pl.ds(6, 1)], incoming[1, q, pl.ds(6, 1)]
        small = (jnp.where(low, first, second) >> own_place) & 3
        code = (jnp.concatenate(parts, axis=0) << 2) | small
        own = code.astype(jnp.float32) * jnp.where(low, unit_of(first), unit_of(second))
        return jnp.where(stay, own, pltpu.roll(pltpu.roll(own, 4, 0), 64, 1))

    def mirror_of(p, h):
        words, last = incoming[h, p, pl.ds(0, 4)], incoming[h, p, pl.ds(6, 1)]
        code = jnp.concatenate([words >> 16, (words << 16) >> 16], axis=0)
        code = (code << 2) | ((last >> mirror_place) & 3)
        return code.astype(jnp.float32) * unit_of(last)

    def finish(q):
        own = own_of(q)
        p = partner[q]
        mirror = mirror_of(p, 0) + mirror_of(p, 1)
        return (own + mirror) * 0.5, pltpu.roll(own - mirror, 4, 0) * sign

    def close(i, carry):
        results = [finish(2 * i), finish(2 * i + 1)]
        start = pl.multiple_of(i * 16, 16)
        plus_ref[pl.ds(start, 16), :] = jnp.concatenate([r[0] for r in results], axis=0).astype(jnp.bfloat16)
        minus_ref[pl.ds(start, 16), :] = jnp.concatenate([r[1] for r in results], axis=0).astype(jnp.bfloat16)
        return carry

    lax.fori_loop(0, 32, close, 0, unroll=2)

    pltpu.make_async_copy(stage.at[0:3], stage.at[0:3], block_send).wait()

    pltpu.make_async_copy(trials.at[0:15], trials.at[0:15], trial_send).wait()

    @pl.when(jnp.logical_not(mine))
    def _():
        pltpu.make_async_copy(trials.at[0], trials.at[0], trial_send).wait()

    @pl.when(mine)
    def _():
        pltpu.make_async_copy(outgoing.at[0:15], outgoing.at[0:15], term_send).wait()
        pltpu.make_async_copy(outgoing.at[0, 0:7], outgoing.at[0, 0:7], term_send).wait()

    @pl.when(jnp.logical_not(mine))
    def _():
        pltpu.make_async_copy(outgoing, outgoing, term_send).wait()


def local(cholesky, trial_rows, occupied, kpoint_map, partner):
    blocks = cholesky.reshape(64, 2, 16, 128)
    trial = trial_rows.reshape(2, 32, 128)
    vmem = pl.BlockSpec(memory_space=pltpu.VMEM)
    bf16, i32 = jnp.bfloat16, jnp.int32
    plus, minus = pl.pallas_call(
        kernel,
        out_shape=[jax.ShapeDtypeStruct((512, 128), bf16)] * 2,
        in_specs=[pl.BlockSpec(memory_space=pl.ANY)] * 5,
        out_specs=[vmem, vmem],
        scratch_shapes=[
            pltpu.VMEM((64, 2, 16, 128), bf16),
            pltpu.VMEM((2, 32, 128), bf16),
            pltpu.VMEM((2, 32, 128), bf16),
            pltpu.SMEM((64,), i32),
            pltpu.SMEM((64, 64), i32),
            pltpu.SMEM((64,), i32),
            pltpu.VMEM((4, 8, 2, 2, 2, 16, 128), bf16),
            pltpu.VMEM((8, 2, 2, 2, 128, 128), bf16),
            pltpu.VMEM((16, 2, 32, 128), bf16),
            pltpu.VMEM((16, 8, 7, 128), i32),
            pltpu.VMEM((2, 64, 7, 128), i32),
            pltpu.SemaphoreType.DMA((5,)),
            pltpu.SemaphoreType.DMA,
            pltpu.SemaphoreType.DMA((8, 4)),
            pltpu.SemaphoreType.DMA,
            pltpu.SemaphoreType.DMA((16,)),
            pltpu.SemaphoreType.DMA,
            pltpu.SemaphoreType.DMA,
        ],
        compiler_params=pltpu.CompilerParams(
            collective_id=0, has_side_effects=True, vmem_limit_bytes=60 * 2**20
        ),
    )(blocks, trial, occupied, kpoint_map, partner)
    shape = (1, 64, 1, 2, 4, 128)
    return plus.reshape(shape), minus.reshape(shape)


def solution(mesh):
    in_specs = (P("pb", None, None, None, "vert", None), P("pb", None, None, None), P(), P(), P())
    out_specs = (P("pb", None, None, None, "vert", None), P("pb", None, None, None, "vert", None))
    return jax.shard_map(local, mesh=mesh, in_specs=in_specs, out_specs=out_specs, check_vma=False)
```

```python
import functools

import jax
import jax.numpy as jnp
from jax import lax
from jax.experimental import pallas as pl
from jax.experimental.pallas import tpu as pltpu
from jax.sharding import PartitionSpec as P

MESH = pl.DeviceIdType.MESH
BITS = 17
TOP = 2**BITS - 1
BIAS = 128


def kpoint(jp, cp, y, zl):
    return jp * 8 + ((y - jp + zl + 8) % 4) * 2 + cp


def encode(own, real, imag):
    peak = jnp.maximum(jnp.maximum(jnp.abs(own), jnp.abs(real)), jnp.abs(imag))
    peak = jnp.max(peak, axis=0, keepdims=True)
    power = jnp.floor(jnp.log2(jnp.maximum(peak, 2.0**-100))) + 1.0
    scale = jnp.exp2(BITS - power)
    biased = (power.astype(jnp.int32) + BIAS) << 24
    row = lax.broadcasted_iota(jnp.int32, (8, 128), 0)
    low = row < 4
    place = (row % 4) * 6

    def code(value, t):
        return jnp.clip(jnp.round(value[8 * t : 8 * t + 8] * scale), -TOP, TOP).astype(jnp.int32)

    messages = []
    for t in range(4):
        a, b, c = code(real, t), code(imag, t), code(own, t)
        mirror = ((a >> 2) << 16) | ((b >> 2) & 65535)
        pairs = ((c >> 2) << 16) | pltpu.roll((c >> 2) & 65535, 6, 0)
        small = (((a & 3) << 4) | ((b & 3) << 2) | (c & 3)) << place
        small = small + pltpu.roll(small, 7, 0)
        small = (small + pltpu.roll(small, 6, 0)) | biased
        rest = jnp.where(row % 4 < 2, pairs, pltpu.roll(small, 2, 0))
        messages.append(jnp.where(low, mirror, pltpu.roll(rest, 4, 0)))
        messages.append(jnp.where(low, pltpu.roll(mirror, 4, 0), rest))
    return messages


def unit_of(word):
    return jnp.exp2((((word >> 24) & 255) - (BIAS + BITS)).astype(jnp.float32))


def kernel(
    blocks_hbm, trial_hbm, occupied_hbm, map_hbm, partner_hbm, plus_ref, minus_ref,
    blocks, trial_ref, masked, occupied, kpoint_map, partner, stage, work, trials, outgoing, incoming, own_terms, mirror_terms,
    plane_in, load_sem, block_send, block_recv, trial_send, trial_recv, term_send, term_recv,
):
    me, v = lax.axis_index("pb"), lax.axis_index("vert")
    zl, x, c = me // 8, (me // 2) % 4, me % 2
    zh, y = v // 4, v % 4
    z = zh * 8 + zl
    mine = x == y
    slot_me = 2 * zl + c
    first_zl = (zl + (y - x + 4) % 4) % 8
    second_zl = (first_zl + 4) % 8

    loads = [
        pltpu.make_async_copy(a, b, load_sem.at[n])
        for n, (a, b) in enumerate(
            [(blocks_hbm, blocks), (trial_hbm, trial_ref), (occupied_hbm, occupied), (map_hbm, kpoint_map), (partner_hbm, partner)]
        )
    ]
    for load in loads:
        load.start()

    barrier = pltpu.get_barrier_semaphore()

    def greet(pb, vert):
        pl.semaphore_signal(barrier, inc=1, device_id=(pb, vert), device_id_type=MESH)

    def greet_ring(i, carry):
        there = (z + i) % 16
        greet((there % 8) * 8 + x * 2 + c, (there // 8) * 4 + y)
        return carry

    def greet_plane(i, carry):
        greet(zl * 8 + ((x + i // 8) % 4) * 2 + (c + i) % 2, zh * 4 + (y + i // 2) % 4)
        return carry

    lax.fori_loop(1, 16, greet_ring, 0, unroll=True)
    lax.fori_loop(1, 32, greet_plane, 0, unroll=True)

    away = pl.multiple_of((1 - zh) * 64, 64)

    def clear(jp, carry):
        for cp in range(2):
            for part in range(2):
                work[jp, cp, 1, part, pl.ds(away, 64), :] = jnp.zeros((64, 128), jnp.bfloat16)
        return carry

    lax.fori_loop(0, 8, clear, 0)
    for load in loads:
        load.wait()

    live = lax.broadcasted_iota(jnp.int32, (32, 128), 0) < occupied[me]
    for part in range(2):
        value = trial_ref[part].astype(jnp.float32)
        masked[part] = jnp.where(live, value, 0.0).astype(jnp.bfloat16)

    @pl.when(mine)
    def _():
        trials[slot_me] = masked[...]

    mirror_q = partner[me]

    def arrange(jp, carry):
        for to in range(4):
            for cp in range(2):
                k = kpoint(jp, cp, to, zl)
                stage[to, jp, cp, 0, 0] = blocks[k, 0]
                stage[to, jp, cp, 0, 1] = -blocks[k, 1]
                stage[to, jp, cp, 1] = blocks[kpoint_map[mirror_q, k]]
        return carry

    lax.fori_loop(0, 8, arrange, 0)

    pl.semaphore_wait(barrier, 46)

    def tell_ring(i, carry):
        there = (z + i) % 16
        pl.semaphore_signal(
            plane_in, inc=1, device_id=((there % 8) * 8 + x * 2 + c, (there // 8) * 4 + y), device_id_type=MESH
        )
        return carry

    lax.fori_loop(1, 16, tell_ring, 0, unroll=True)

    def rows_from(jp, source):
        start = pl.multiple_of(zh * 64 + source * 16, 16)
        return work.at[jp, :, :, :, pl.ds(start, 16), :]

    def block_copy(i, d, source, target):
        jp = (zl + i) % 8
        return pltpu.make_async_remote_copy(
            src_ref=stage.at[target, jp],
            dst_ref=rows_from(jp, source),
            send_sem=block_send,
            recv_sem=block_recv.at[i, d],
            device_id=(me, zh * 4 + target),
            device_id_type=MESH,
        )

    def self_copy(i):
        jp = (zl + i) % 8
        return pltpu.make_async_copy(stage.at[y, jp], rows_from(jp, y), block_recv.at[i, 0])

    def trial_copy(slot, pb, vert, source=None):
        return pltpu.make_async_remote_copy(
            src_ref=trials.at[slot] if source is None else source,
            dst_ref=trials.at[slot],
            send_sem=trial_send,
            recv_sem=trial_recv.at[slot],
            device_id=(pb, vert),
            device_id_type=MESH,
        )

    def forward(there):
        for i in range(1, 8):
            trial_copy(2 * there + c, zl * 8 + ((x + i // 2) % 4) * 2 + (c + i) % 2, v).start()

    def block_sends(i, carry):
        self_copy(i).start()
        for d in range(1, 4):
            block_copy(i, d, y, (y + d) % 4).start()
        return carry

    block_sends(0, 0)

    def trial_along(d):
        there = (z - d + 16) % 16
        trial_copy(slot_me, (there % 8) * 8 + x * 2 + c, (there // 8) * 4 + y, masked).start()

    offset = (y - x + 4) % 4

    @pl.when(mine)
    def _():
        forward(zl)

    @pl.when(jnp.logical_not(mine))
    def _():
        trial_along(offset)

    trial_along(offset - 4)
    lax.fori_loop(1, 8, block_sends, 0, unroll=True)

    @pl.when(jnp.logical_not(mine))
    def _():
        trial_copy(2 * first_zl + c, me, v).wait_recv()
        forward(first_zl)


    trial_copy(2 * second_zl + c, me, v).wait_recv()
    forward(second_zl)

    here = pl.multiple_of(zh * 64, 64)
    low = lax.broadcasted_iota(jnp.int32, (8, 128), 0) < 4

    def terms(i, carry):
        jp = (zl + i) % 8


        self_copy(i).wait()
        for d in range(1, 4):
            block_copy(i, d, (y - d + 4) % 4, y).wait_recv()
        for cp in range(2):
            slot = 2 * jp + cp

            @pl.when((cp != c) | ((jp != first_zl) & (jp != second_zl)))
            def _():
                trial_copy(slot, me, v).wait_recv()

            real, imag = trials[slot, 0], trials[slot, 1]
            left = jnp.concatenate(
                [jnp.concatenate([real, imag], axis=1), jnp.concatenate([imag, -real], axis=1)], axis=0
            )
            mirror = jnp.dot(left, work[jp, cp, 1].reshape(256, 128), preferred_element_type=jnp.float32)
            right = jnp.concatenate(
                [work[jp, cp, 0, 0, pl.ds(here, 64), :], work[jp, cp, 0, 1, pl.ds(here, 64), :]], axis=1
            )
            own = lax.dot_general(
                left, right, (((1,), (1,)), ((), ())), preferred_element_type=jnp.float32
            )
            own = jnp.concatenate([own[:32], own[32:]], axis=1)
            messages = encode(own, mirror[:32], mirror[32:])
            k = kpoint(jp, cp, y, zl)
            for w in range(8):
                outgoing[slot, w] = messages[w][:7]
            if cp == 0:

                @pl.when(i == 0)
                def _():
                    pl.semaphore_wait(plane_in, 15)

            for w in range(8):
                own_tile = (k == me) & (w == v)

                @pl.when(own_tile)
                def _():
                    pltpu.make_async_copy(outgoing.at[slot, w], incoming.at[zh, me], term_recv.at[zl]).start()

                @pl.when(jnp.logical_not(own_tile))
                def _():
                    pltpu.make_async_remote_copy(
                        src_ref=outgoing.at[slot, w],
                        dst_ref=incoming.at[zh, me],
                        send_sem=term_send,
                        recv_sem=term_recv.at[zl],
                        device_id=(k, w),
                        device_id_type=MESH,
                    ).start()

        return carry

    lax.fori_loop(0, 8, terms, 0)

    lane = lax.broadcasted_iota(jnp.int32, (8, 128), 1) < 64
    stay = low == lane
    sign = jnp.where(low, 0.5, -0.5)

    row = lax.broadcasted_iota(jnp.int32, (8, 128), 0)
    own_place = (row % 4) * 6
    mirror_place = own_place + jnp.where(low, 4, 2)

    def own_of(q):
        parts = []
        for h in range(2):
            pairs = incoming[h, q, pl.ds(4, 2)]
            parts += [pairs >> 16, (pairs << 16) >> 16]
        first, second = incoming[0, q, pl.ds(6, 1)], incoming[1, q, pl.ds(6, 1)]
        small = (jnp.where(low, first, second) >> own_place) & 3
        code = (jnp.concatenate(parts, axis=0) << 2) | small
        own = code.astype(jnp.float32) * jnp.where(low, unit_of(first), unit_of(second))
        return jnp.where(stay, own, pltpu.roll(pltpu.roll(own, 4, 0), 64, 1))

    def mirror_of(p, h):
        words, last = incoming[h, p, pl.ds(0, 4)], incoming[h, p, pl.ds(6, 1)]
        code = jnp.concatenate([words >> 16, (words << 16) >> 16], axis=0)
        code = (code << 2) | ((last >> mirror_place) & 3)
        return code.astype(jnp.float32) * unit_of(last)

    def decode(o, carry):
        start = pl.multiple_of((zl - o + 8) % 8 * 8, 8)
        part = incoming.at[:, pl.ds(start, 8)]
        pltpu.make_async_copy(part, part, term_recv.at[(zl - o + 8) % 8]).wait()

        def one(n, carry):
            q = start + n
            own_terms[q] = own_of(q)
            mirror_terms[q] = mirror_of(q, 0) + mirror_of(q, 1)
            return carry

        return lax.fori_loop(0, 8, one, carry, unroll=4)

    lax.fori_loop(0, 8, decode, 0)

    def finish(q):
        own, mirror = own_terms[q], mirror_terms[partner[q]]
        return (own + mirror) * 0.5, pltpu.roll(own - mirror, 4, 0) * sign

    def close(i, carry):
        results = [finish(2 * i), finish(2 * i + 1)]
        start = pl.multiple_of(i * 16, 16)
        plus_ref[pl.ds(start, 16), :] = jnp.concatenate([r[0] for r in results], axis=0).astype(jnp.bfloat16)
        minus_ref[pl.ds(start, 16), :] = jnp.concatenate([r[1] for r in results], axis=0).astype(jnp.bfloat16)
        return carry

    lax.fori_loop(0, 32, close, 0, unroll=4)

    pltpu.make_async_copy(stage.at[0:3], stage.at[0:3], block_send).wait()

    pltpu.make_async_copy(trials.at[0:15], trials.at[0:15], trial_send).wait()

    @pl.when(jnp.logical_not(mine))
    def _():
        pltpu.make_async_copy(trials.at[0], trials.at[0], trial_send).wait()

    @pl.when(mine)
    def _():
        pltpu.make_async_copy(outgoing.at[0:15], outgoing.at[0:15], term_send).wait()
        pltpu.make_async_copy(outgoing.at[0, 0:7], outgoing.at[0, 0:7], term_send).wait()

    @pl.when(jnp.logical_not(mine))
    def _():
        pltpu.make_async_copy(outgoing, outgoing, term_send).wait()


def local(cholesky, trial_rows, occupied, kpoint_map, partner):
    blocks = cholesky.reshape(64, 2, 16, 128)
    trial = trial_rows.reshape(2, 32, 128)
    vmem = pl.BlockSpec(memory_space=pltpu.VMEM)
    bf16, i32 = jnp.bfloat16, jnp.int32
    plus, minus = pl.pallas_call(
        kernel,
        out_shape=[jax.ShapeDtypeStruct((512, 128), bf16)] * 2,
        in_specs=[pl.BlockSpec(memory_space=pl.ANY)] * 5,
        out_specs=[vmem, vmem],
        scratch_shapes=[
            pltpu.VMEM((64, 2, 16, 128), bf16),
            pltpu.VMEM((2, 32, 128), bf16),
            pltpu.VMEM((2, 32, 128), bf16),
            pltpu.SMEM((64,), i32),
            pltpu.SMEM((64, 64), i32),
            pltpu.SMEM((64,), i32),
            pltpu.VMEM((4, 8, 2, 2, 2, 16, 128), bf16),
            pltpu.VMEM((8, 2, 2, 2, 128, 128), bf16),
            pltpu.VMEM((16, 2, 32, 128), bf16),
            pltpu.VMEM((16, 8, 7, 128), i32),
            pltpu.VMEM((2, 64, 7, 128), i32),
            pltpu.VMEM((64, 8, 128), jnp.float32),
            pltpu.VMEM((64, 8, 128), jnp.float32),
            pltpu.SemaphoreType.REGULAR,
            pltpu.SemaphoreType.DMA((5,)),
            pltpu.SemaphoreType.DMA,
            pltpu.SemaphoreType.DMA((8, 4)),
            pltpu.SemaphoreType.DMA,
            pltpu.SemaphoreType.DMA((16,)),
            pltpu.SemaphoreType.DMA,
            pltpu.SemaphoreType.DMA((8,)),
        ],
        compiler_params=pltpu.CompilerParams(
            collective_id=0, has_side_effects=True, vmem_limit_bytes=32 * 2**20
        ),
    )(*[pltpu.with_memory_space_constraint(a, pltpu.HBM) for a in (blocks, trial, occupied, kpoint_map, partner)])
    shape = (1, 64, 1, 2, 4, 128)
    return plus.reshape(shape), minus.reshape(shape)


def solution(mesh):
    in_specs = (P("pb", None, None, None, "vert", None), P("pb", None, None, None), P(), P(), P())
    out_specs = (P("pb", None, None, None, "vert", None), P("pb", None, None, None, "vert", None))
    return jax.shard_map(local, mesh=mesh, in_specs=in_specs, out_specs=out_specs, check_vma=False)
```

```python
import functools

import jax
import jax.numpy as jnp
from jax import lax
from jax.experimental import pallas as pl
from jax.experimental.pallas import tpu as pltpu
from jax.sharding import PartitionSpec as P

MESH = pl.DeviceIdType.MESH
BITS = 17
TOP = 2**BITS - 1
BIAS = 128


def kpoint(jp, cp, y, zl):
    return jp * 8 + ((y - jp + zl + 8) % 4) * 2 + cp


def encode(own, real, imag):
    peak = jnp.maximum(jnp.maximum(jnp.abs(own), jnp.abs(real)), jnp.abs(imag))
    peak = jnp.max(peak, axis=0, keepdims=True)
    power = jnp.floor(jnp.log2(jnp.maximum(peak, 2.0**-100))) + 1.0
    scale = jnp.exp2(BITS - power)
    biased = (power.astype(jnp.int32) + BIAS) << 24
    row = lax.broadcasted_iota(jnp.int32, (8, 128), 0)
    low = row < 4
    place = (row % 4) * 6

    def code(value, t):
        return jnp.clip(jnp.round(value[8 * t : 8 * t + 8] * scale), -TOP, TOP).astype(jnp.int32)

    messages = []
    for t in range(4):
        a, b, c = code(real, t), code(imag, t), code(own, t)
        mirror = ((a >> 2) << 16) | ((b >> 2) & 65535)
        pairs = ((c >> 2) << 16) | pltpu.roll((c >> 2) & 65535, 6, 0)
        small = (((a & 3) << 4) | ((b & 3) << 2) | (c & 3)) << place
        small = small + pltpu.roll(small, 7, 0)
        small = (small + pltpu.roll(small, 6, 0)) | biased
        rest = jnp.where(row % 4 < 2, pairs, pltpu.roll(small, 2, 0))
        messages.append(jnp.where(low, mirror, pltpu.roll(rest, 4, 0)))
        messages.append(jnp.where(low, pltpu.roll(mirror, 4, 0), rest))
    return messages


def unit_of(word):
    return jnp.exp2((((word >> 24) & 255) - (BIAS + BITS)).astype(jnp.float32))


def kernel(
    blocks_hbm, trial_hbm, occupied_hbm, map_hbm, partner_hbm, plus_ref, minus_ref,
    blocks, trial_ref, masked, occupied, kpoint_map, partner, stage, work, trials, outgoing, incoming, own_terms, mirror_terms,
    plane_in, load_sem, block_send, block_recv, trial_send, trial_recv, term_send, term_recv,
):
    me, v = lax.axis_index("pb"), lax.axis_index("vert")
    zl, x, c = me // 8, (me // 2) % 4, me % 2
    zh, y = v // 4, v % 4
    z = zh * 8 + zl
    mine = x == y
    slot_me = 2 * zl + c
    offset = (y - x + 4) % 4
    first_zl = (zl + offset + 4 * (offset // 3)) % 8
    second_zl = (first_zl + 4) % 8

    loads = [
        pltpu.make_async_copy(a, b, load_sem.at[n])
        for n, (a, b) in enumerate(
            [(blocks_hbm, blocks), (trial_hbm, trial_ref), (occupied_hbm, occupied), (map_hbm, kpoint_map), (partner_hbm, partner)]
        )
    ]
    for load in loads:
        load.start()

    barrier = pltpu.get_barrier_semaphore()

    def greet(pb, vert):
        pl.semaphore_signal(barrier, inc=1, device_id=(pb, vert), device_id_type=MESH)

    def greet_ring(i, carry):
        there = (z + i) % 16
        greet((there % 8) * 8 + x * 2 + c, (there // 8) * 4 + y)
        return carry

    def greet_plane(i, carry):
        greet(zl * 8 + ((x + i // 8) % 4) * 2 + (c + i) % 2, zh * 4 + (y + i // 2) % 4)
        return carry

    lax.fori_loop(1, 16, greet_ring, 0, unroll=True)
    lax.fori_loop(1, 32, greet_plane, 0, unroll=True)

    away = pl.multiple_of((1 - zh) * 64, 64)

    def clear(jp, carry):
        for cp in range(2):
            for part in range(2):
                work[jp, cp, 1, part, pl.ds(away, 64), :] = jnp.zeros((64, 128), jnp.bfloat16)
        return carry

    lax.fori_loop(0, 8, clear, 0)
    for load in loads:
        load.wait()

    live = lax.broadcasted_iota(jnp.int32, (32, 128), 0) < occupied[me]
    for part in range(2):
        value = trial_ref[part].astype(jnp.float32)
        masked[part] = jnp.where(live, value, 0.0).astype(jnp.bfloat16)

    @pl.when(mine)
    def _():
        trials[slot_me] = masked[...]

    mirror_q = partner[me]

    def arrange(jp, carry):
        for to in range(4):
            for cp in range(2):
                k = kpoint(jp, cp, to, zl)
                stage[to, jp, cp, 0, 0] = blocks[k, 0]
                stage[to, jp, cp, 0, 1] = -blocks[k, 1]
                stage[to, jp, cp, 1] = blocks[kpoint_map[mirror_q, k]]
        return carry

    lax.fori_loop(0, 8, arrange, 0)

    pl.semaphore_wait(barrier, 46)

    def tell_ring(i, carry):
        there = (z + i) % 16
        pl.semaphore_signal(
            plane_in, inc=1, device_id=((there % 8) * 8 + x * 2 + c, (there // 8) * 4 + y), device_id_type=MESH
        )
        return carry

    lax.fori_loop(1, 16, tell_ring, 0, unroll=True)

    def plane_at(i, sign=1):
        return (zl + sign * ((i + 1) // 2) * (2 * (i % 2) - 1) + 8) % 8

    def rows_from(jp, source):
        start = pl.multiple_of(zh * 64 + source * 16, 16)
        return work.at[jp, :, :, :, pl.ds(start, 16), :]

    def block_copy(i, d, source, target):
        jp = plane_at(i)
        return pltpu.make_async_remote_copy(
            src_ref=stage.at[target, jp],
            dst_ref=rows_from(jp, source),
            send_sem=block_send,
            recv_sem=block_recv.at[i, d],
            device_id=(me, zh * 4 + target),
            device_id_type=MESH,
        )

    def self_copy(i):
        jp = plane_at(i)
        return pltpu.make_async_copy(stage.at[y, jp], rows_from(jp, y), block_recv.at[i, 0])

    def trial_copy(slot, pb, vert, source=None):
        return pltpu.make_async_remote_copy(
            src_ref=trials.at[slot] if source is None else source,
            dst_ref=trials.at[slot],
            send_sem=trial_send,
            recv_sem=trial_recv.at[slot],
            device_id=(pb, vert),
            device_id_type=MESH,
        )

    def forward(there):
        for i in range(1, 8):
            trial_copy(2 * there + c, zl * 8 + ((x + i // 2) % 4) * 2 + (c + i) % 2, v).start()

    def block_sends(i, carry):
        self_copy(i).start()
        for d in range(1, 4):
            block_copy(i, d, y, (y + d) % 4).start()
        return carry

    block_sends(0, 0)

    def trial_along(d):
        there = (z - d + 16) % 16
        trial_copy(slot_me, (there % 8) * 8 + x * 2 + c, (there // 8) * 4 + y, masked).start()

    @pl.when(mine)
    def _():
        forward(zl)

    @pl.when(jnp.logical_not(mine))
    def _():
        trial_along(offset)

    trial_along(offset - 4)
    lax.fori_loop(1, 8, block_sends, 0, unroll=True)

    @pl.when(jnp.logical_not(mine))
    def _():
        trial_copy(2 * first_zl + c, me, v).wait_recv()
        forward(first_zl)


    trial_copy(2 * second_zl + c, me, v).wait_recv()
    forward(second_zl)

    here = pl.multiple_of(zh * 64, 64)
    low = lax.broadcasted_iota(jnp.int32, (8, 128), 0) < 4

    def terms(i, carry):
        jp = plane_at(i)


        self_copy(i).wait()
        for d in range(1, 4):
            block_copy(i, d, (y - d + 4) % 4, y).wait_recv()
        for cp in range(2):
            slot = 2 * jp + cp

            @pl.when((cp != c) | ((jp != first_zl) & (jp != second_zl)))
            def _():
                trial_copy(slot, me, v).wait_recv()

            real, imag = trials[slot, 0], trials[slot, 1]
            left = jnp.concatenate(
                [jnp.concatenate([real, imag], axis=1), jnp.concatenate([imag, -real], axis=1)], axis=0
            )
            mirror = jnp.dot(left, work[jp, cp, 1].reshape(256, 128), preferred_element_type=jnp.float32)
            right = jnp.concatenate(
                [work[jp, cp, 0, 0, pl.ds(here, 64), :], work[jp, cp, 0, 1, pl.ds(here, 64), :]], axis=1
            )
            own = lax.dot_general(
                left, right, (((1,), (1,)), ((), ())), preferred_element_type=jnp.float32
            )
            own = jnp.concatenate([own[:32], own[32:]], axis=1)
            messages = encode(own, mirror[:32], mirror[32:])
            k = kpoint(jp, cp, y, zl)
            for w in range(8):
                outgoing[slot, w] = messages[w][:7]
            if cp == 0:

                @pl.when(i == 0)
                def _():
                    pl.semaphore_wait(plane_in, 15)

            for w in range(8):
                own_tile = (k == me) & (w == v)

                @pl.when(own_tile)
                def _():
                    pltpu.make_async_copy(outgoing.at[slot, w], incoming.at[zh, me], term_recv.at[zl]).start()

                @pl.when(jnp.logical_not(own_tile))
                def _():
                    pltpu.make_async_remote_copy(
                        src_ref=outgoing.at[slot, w],
                        dst_ref=incoming.at[zh, me],
                        send_sem=term_send,
                        recv_sem=term_recv.at[zl],
                        device_id=(k, w),
                        device_id_type=MESH,
                    ).start()

        return carry

    lax.fori_loop(0, 8, terms, 0)

    lane = lax.broadcasted_iota(jnp.int32, (8, 128), 1) < 64
    stay = low == lane
    sign = jnp.where(low, 0.5, -0.5)

    row = lax.broadcasted_iota(jnp.int32, (8, 128), 0)
    own_place = (row % 4) * 6
    mirror_place = own_place + jnp.where(low, 4, 2)

    def own_of(q):
        parts = []
        for h in range(2):
            pairs = incoming[h, q, pl.ds(4, 2)]
            parts += [pairs >> 16, (pairs << 16) >> 16]
        first, second = incoming[0, q, pl.ds(6, 1)], incoming[1, q, pl.ds(6, 1)]
        small = (jnp.where(low, first, second) >> own_place) & 3
        code = (jnp.concatenate(parts, axis=0) << 2) | small
        own = code.astype(jnp.float32) * jnp.where(low, unit_of(first), unit_of(second))
        return jnp.where(stay, own, pltpu.roll(pltpu.roll(own, 4, 0), 64, 1))

    def mirror_of(p, h):
        words, last = incoming[h, p, pl.ds(0, 4)], incoming[h, p, pl.ds(6, 1)]
        code = jnp.concatenate([words >> 16, (words << 16) >> 16], axis=0)
        code = (code << 2) | ((last >> mirror_place) & 3)
        return code.astype(jnp.float32) * unit_of(last)

    def decode(o, carry):
        plane = plane_at(o, -1)
        start = pl.multiple_of(plane * 8, 8)
        part = incoming.at[:, pl.ds(start, 8)]
        pltpu.make_async_copy(part, part, term_recv.at[plane]).wait()

        def one(n, carry):
            q = start + n
            own_terms[q] = own_of(q)
            mirror_terms[q] = mirror_of(q, 0) + mirror_of(q, 1)
            return carry

        return lax.fori_loop(0, 8, one, carry, unroll=4)

    lax.fori_loop(0, 8, decode, 0)

    def finish(q):
        own, mirror = own_terms[q], mirror_terms[partner[q]]
        return (own + mirror) * 0.5, pltpu.roll(own - mirror, 4, 0) * sign

    def close(i, carry):
        results = [finish(2 * i), finish(2 * i + 1)]
        start = pl.multiple_of(i * 16, 16)
        plus_ref[pl.ds(start, 16), :] = jnp.concatenate([r[0] for r in results], axis=0).astype(jnp.bfloat16)
        minus_ref[pl.ds(start, 16), :] = jnp.concatenate([r[1] for r in results], axis=0).astype(jnp.bfloat16)
        return carry

    lax.fori_loop(0, 32, close, 0, unroll=4)

    pltpu.make_async_copy(stage.at[0:3], stage.at[0:3], block_send).wait()

    pltpu.make_async_copy(trials.at[0:15], trials.at[0:15], trial_send).wait()

    @pl.when(jnp.logical_not(mine))
    def _():
        pltpu.make_async_copy(trials.at[0], trials.at[0], trial_send).wait()

    @pl.when(mine)
    def _():
        pltpu.make_async_copy(outgoing.at[0:15], outgoing.at[0:15], term_send).wait()
        pltpu.make_async_copy(outgoing.at[0, 0:7], outgoing.at[0, 0:7], term_send).wait()

    @pl.when(jnp.logical_not(mine))
    def _():
        pltpu.make_async_copy(outgoing, outgoing, term_send).wait()


def local(cholesky, trial_rows, occupied, kpoint_map, partner):
    blocks = cholesky.reshape(64, 2, 16, 128)
    trial = trial_rows.reshape(2, 32, 128)
    vmem = pl.BlockSpec(memory_space=pltpu.VMEM)
    bf16, i32 = jnp.bfloat16, jnp.int32
    plus, minus = pl.pallas_call(
        kernel,
        out_shape=[jax.ShapeDtypeStruct((512, 128), bf16)] * 2,
        in_specs=[pl.BlockSpec(memory_space=pl.ANY)] * 5,
        out_specs=[vmem, vmem],
        scratch_shapes=[
            pltpu.VMEM((64, 2, 16, 128), bf16),
            pltpu.VMEM((2, 32, 128), bf16),
            pltpu.VMEM((2, 32, 128), bf16),
            pltpu.SMEM((64,), i32),
            pltpu.SMEM((64, 64), i32),
            pltpu.SMEM((64,), i32),
            pltpu.VMEM((4, 8, 2, 2, 2, 16, 128), bf16),
            pltpu.VMEM((8, 2, 2, 2, 128, 128), bf16),
            pltpu.VMEM((16, 2, 32, 128), bf16),
            pltpu.VMEM((16, 8, 7, 128), i32),
            pltpu.VMEM((2, 64, 7, 128), i32),
            pltpu.VMEM((64, 8, 128), jnp.float32),
            pltpu.VMEM((64, 8, 128), jnp.float32),
            pltpu.SemaphoreType.REGULAR,
            pltpu.SemaphoreType.DMA((5,)),
            pltpu.SemaphoreType.DMA,
            pltpu.SemaphoreType.DMA((8, 4)),
            pltpu.SemaphoreType.DMA,
            pltpu.SemaphoreType.DMA((16,)),
            pltpu.SemaphoreType.DMA,
            pltpu.SemaphoreType.DMA((8,)),
        ],
        compiler_params=pltpu.CompilerParams(
            collective_id=0, has_side_effects=True, vmem_limit_bytes=32 * 2**20
        ),
    )(*[pltpu.with_memory_space_constraint(a, pltpu.HBM) for a in (blocks, trial, occupied, kpoint_map, partner)])
    shape = (1, 64, 1, 2, 4, 128)
    return plus.reshape(shape), minus.reshape(shape)


def solution(mesh):
    in_specs = (P("pb", None, None, None, "vert", None), P("pb", None, None, None), P(), P(), P())
    out_specs = (P("pb", None, None, None, "vert", None), P("pb", None, None, None, "vert", None))
    return jax.shard_map(local, mesh=mesh, in_specs=in_specs, out_specs=out_specs, check_vma=False)
```

```python
import functools

import jax
import jax.numpy as jnp
from jax import lax
from jax.experimental import pallas as pl
from jax.experimental.pallas import tpu as pltpu
from jax.sharding import PartitionSpec as P

MESH = pl.DeviceIdType.MESH
BITS = 17
TOP = 2**BITS - 1
BIAS = 128


def kpoint(jp, cp, y, zl):
    return jp * 8 + ((y - jp + zl + 8) % 4) * 2 + cp


def encode(own, real, imag):
    peak = jnp.maximum(jnp.maximum(jnp.abs(own), jnp.abs(real)), jnp.abs(imag))
    peak = jnp.max(peak, axis=0, keepdims=True)
    power = jnp.floor(jnp.log2(jnp.maximum(peak, 2.0**-100))) + 1.0
    scale = jnp.exp2(BITS - power)
    biased = (power.astype(jnp.int32) + BIAS) << 24
    row = lax.broadcasted_iota(jnp.int32, (8, 128), 0)
    low = row < 4
    place = (row % 4) * 6

    def code(value, t):
        return jnp.clip(jnp.round(value[8 * t : 8 * t + 8] * scale), -TOP, TOP).astype(jnp.int32)

    messages = []
    for t in range(4):
        a, b, c = code(real, t), code(imag, t), code(own, t)
        mirror = ((a >> 2) << 16) | ((b >> 2) & 65535)
        pairs = ((c >> 2) << 16) | pltpu.roll((c >> 2) & 65535, 6, 0)
        small = (((a & 3) << 4) | ((b & 3) << 2) | (c & 3)) << place
        small = small + pltpu.roll(small, 7, 0)
        small = (small + pltpu.roll(small, 6, 0)) | biased
        rest = jnp.where(row % 4 < 2, pairs, pltpu.roll(small, 2, 0))
        messages.append(jnp.where(low, mirror, pltpu.roll(rest, 4, 0)))
        messages.append(jnp.where(low, pltpu.roll(mirror, 4, 0), rest))
    return messages


def unit_of(word):
    return jnp.exp2((((word >> 24) & 255) - (BIAS + BITS)).astype(jnp.float32))


def kernel(
    blocks_hbm, trial_hbm, occupied_hbm, map_hbm, partner_hbm, plus_ref, minus_ref,
    blocks, trial_ref, masked, occupied, kpoint_map, partner, stage, work, trials, outgoing, incoming, own_terms, mirror_terms,
    plane_in, load_sem, block_send, block_recv, trial_send, trial_recv, term_send, term_recv,
):
    me, v = lax.axis_index("pb"), lax.axis_index("vert")
    zl, x, c = me // 8, (me // 2) % 4, me % 2
    zh, y = v // 4, v % 4
    z = zh * 8 + zl
    mine = x == y
    slot_me = 2 * zl + c
    offset = (y - x + 4) % 4
    first_zl = (zl + offset + 4 * (offset // 3)) % 8
    second_zl = (first_zl + 4) % 8

    loads = [
        pltpu.make_async_copy(a, b, load_sem.at[n])
        for n, (a, b) in enumerate(
            [(blocks_hbm, blocks), (trial_hbm, trial_ref), (occupied_hbm, occupied), (map_hbm, kpoint_map), (partner_hbm, partner)]
        )
    ]
    for load in loads:
        load.start()

    barrier = pltpu.get_barrier_semaphore()

    def greet(pb, vert):
        pl.semaphore_signal(barrier, inc=1, device_id=(pb, vert), device_id_type=MESH)

    def greet_ring(i, carry):
        there = (z + i) % 16
        greet((there % 8) * 8 + x * 2 + c, (there // 8) * 4 + y)
        return carry

    def greet_plane(i, carry):
        greet(zl * 8 + ((x + i // 8) % 4) * 2 + (c + i) % 2, zh * 4 + (y + i // 2) % 4)
        return carry

    for n, i in enumerate((8, 7, 9, 6, 10, 5, 11, 4, 12, 3, 13, 2, 14, 1, 15)):
        greet_ring(i, 0)
        greet_plane(2 * n + 1, 0)
        greet_plane(2 * n + 2, 0)
    greet_plane(31, 0)

    away = pl.multiple_of((1 - zh) * 64, 64)

    def clear(jp, carry):
        for cp in range(2):
            for part in range(2):
                work[jp, cp, 1, part, pl.ds(away, 64), :] = jnp.zeros((64, 128), jnp.bfloat16)
        return carry

    lax.fori_loop(0, 8, clear, 0)
    for load in loads:
        load.wait()

    live = lax.broadcasted_iota(jnp.int32, (32, 128), 0) < occupied[me]
    for part in range(2):
        value = trial_ref[part].astype(jnp.float32)
        masked[part] = jnp.where(live, value, 0.0).astype(jnp.bfloat16)

    @pl.when(mine)
    def _():
        trials[slot_me] = masked[...]

    mirror_q = partner[me]

    def arrange(jp, carry):
        for to in range(4):
            for cp in range(2):
                k = kpoint(jp, cp, to, zl)
                stage[to, jp, cp, 0, 0] = blocks[k, 0]
                stage[to, jp, cp, 0, 1] = -blocks[k, 1]
                stage[to, jp, cp, 1] = blocks[kpoint_map[mirror_q, k]]
        return carry

    lax.fori_loop(0, 8, arrange, 0)

    pl.semaphore_wait(barrier, 46)

    def tell_ring(i, carry):
        there = (z + i) % 16
        pl.semaphore_signal(
            plane_in, inc=1, device_id=((there % 8) * 8 + x * 2 + c, (there // 8) * 4 + y), device_id_type=MESH
        )
        return carry

    for i in (8, 7, 9, 6, 10, 5, 11, 4, 12, 3, 13, 2, 14, 1, 15):
        tell_ring(i, 0)

    def plane_at(i, sign=1):
        return (zl + sign * ((i + 1) // 2) * (2 * (i % 2) - 1) + 8) % 8

    def rows_from(jp, source):
        start = pl.multiple_of(zh * 64 + source * 16, 16)
        return work.at[jp, :, :, :, pl.ds(start, 16), :]

    def block_copy(i, d, source, target):
        jp = plane_at(i)
        return pltpu.make_async_remote_copy(
            src_ref=stage.at[target, jp],
            dst_ref=rows_from(jp, source),
            send_sem=block_send,
            recv_sem=block_recv.at[i, d],
            device_id=(me, zh * 4 + target),
            device_id_type=MESH,
        )

    def self_copy(i):
        jp = plane_at(i)
        return pltpu.make_async_copy(stage.at[y, jp], rows_from(jp, y), block_recv.at[i, 0])

    def trial_copy(slot, pb, vert, source=None):
        return pltpu.make_async_remote_copy(
            src_ref=trials.at[slot] if source is None else source,
            dst_ref=trials.at[slot],
            send_sem=trial_send,
            recv_sem=trial_recv.at[slot],
            device_id=(pb, vert),
            device_id_type=MESH,
        )

    def forward(there):
        for i in range(1, 8):
            trial_copy(2 * there + c, zl * 8 + ((x + i // 2) % 4) * 2 + (c + i) % 2, v).start()

    def block_sends(i, carry):
        self_copy(i).start()
        for d in range(1, 4):
            block_copy(i, d, y, (y + d) % 4).start()
        return carry

    block_sends(0, 0)

    def trial_along(d):
        there = (z - d + 16) % 16
        trial_copy(slot_me, (there % 8) * 8 + x * 2 + c, (there // 8) * 4 + y, masked).start()

    @pl.when(mine)
    def _():
        forward(zl)

    @pl.when(jnp.logical_not(mine))
    def _():
        trial_along(offset)

    trial_along(offset - 4)
    lax.fori_loop(1, 8, block_sends, 0, unroll=True)

    @pl.when(jnp.logical_not(mine))
    def _():
        trial_copy(2 * first_zl + c, me, v).wait_recv()
        forward(first_zl)


    here = pl.multiple_of(zh * 64, 64)
    low = lax.broadcasted_iota(jnp.int32, (8, 128), 0) < 4

    def terms(i, carry):
        jp = plane_at(i)

        @pl.when(i == 2)
        def _():
            trial_copy(2 * second_zl + c, me, v).wait_recv()
            forward(second_zl)

        self_copy(i).wait()
        for d in range(1, 4):
            block_copy(i, d, (y - d + 4) % 4, y).wait_recv()
        for cp in range(2):
            slot = 2 * jp + cp

            @pl.when((cp != c) | ((jp != first_zl) & (jp != second_zl)))
            def _():
                trial_copy(slot, me, v).wait_recv()

            real, imag = trials[slot, 0], trials[slot, 1]
            left = jnp.concatenate(
                [jnp.concatenate([real, imag], axis=1), jnp.concatenate([imag, -real], axis=1)], axis=0
            )
            mirror = jnp.dot(left, work[jp, cp, 1].reshape(256, 128), preferred_element_type=jnp.float32)
            right = jnp.concatenate(
                [work[jp, cp, 0, 0, pl.ds(here, 64), :], work[jp, cp, 0, 1, pl.ds(here, 64), :]], axis=1
            )
            own = lax.dot_general(
                left, right, (((1,), (1,)), ((), ())), preferred_element_type=jnp.float32
            )
            own = jnp.concatenate([own[:32], own[32:]], axis=1)
            messages = encode(own, mirror[:32], mirror[32:])
            k = kpoint(jp, cp, y, zl)
            for w in range(8):
                outgoing[slot, w] = messages[w][:7]
            if cp == 0:

                @pl.when(i == 0)
                def _():
                    pl.semaphore_wait(plane_in, 15)

            for w in range(8):
                own_tile = (k == me) & (w == v)

                @pl.when(own_tile)
                def _():
                    pltpu.make_async_copy(outgoing.at[slot, w], incoming.at[zh, me], term_recv.at[zl]).start()

                @pl.when(jnp.logical_not(own_tile))
                def _():
                    pltpu.make_async_remote_copy(
                        src_ref=outgoing.at[slot, w],
                        dst_ref=incoming.at[zh, me],
                        send_sem=term_send,
                        recv_sem=term_recv.at[zl],
                        device_id=(k, w),
                        device_id_type=MESH,
                    ).start()

        return carry

    lax.fori_loop(0, 8, terms, 0)

    lane = lax.broadcasted_iota(jnp.int32, (8, 128), 1) < 64
    stay = low == lane
    sign = jnp.where(low, 0.5, -0.5)

    row = lax.broadcasted_iota(jnp.int32, (8, 128), 0)
    own_place = (row % 4) * 6
    mirror_place = own_place + jnp.where(low, 4, 2)

    def own_of(q):
        parts = []
        for h in range(2):
            pairs = incoming[h, q, pl.ds(4, 2)]
            parts += [pairs >> 16, (pairs << 16) >> 16]
        first, second = incoming[0, q, pl.ds(6, 1)], incoming[1, q, pl.ds(6, 1)]
        small = (jnp.where(low, first, second) >> own_place) & 3
        code = (jnp.concatenate(parts, axis=0) << 2) | small
        own = code.astype(jnp.float32) * jnp.where(low, unit_of(first), unit_of(second))
        return jnp.where(stay, own, pltpu.roll(pltpu.roll(own, 4, 0), 64, 1))

    def mirror_of(p, h):
        words, last = incoming[h, p, pl.ds(0, 4)], incoming[h, p, pl.ds(6, 1)]
        code = jnp.concatenate([words >> 16, (words << 16) >> 16], axis=0)
        code = (code << 2) | ((last >> mirror_place) & 3)
        return code.astype(jnp.float32) * unit_of(last)

    def decode(o, carry):
        plane = plane_at(o, -1)
        start = pl.multiple_of(plane * 8, 8)
        part = incoming.at[:, pl.ds(start, 8)]
        pltpu.make_async_copy(part, part, term_recv.at[plane]).wait()

        def one(n, carry):
            q = start + n
            own_terms[q] = own_of(q)
            mirror_terms[q] = mirror_of(q, 0) + mirror_of(q, 1)
            return carry

        return lax.fori_loop(0, 8, one, carry, unroll=4)

    lax.fori_loop(0, 8, decode, 0)

    def finish(q):
        own, mirror = own_terms[q], mirror_terms[partner[q]]
        return (own + mirror) * 0.5, pltpu.roll(own - mirror, 4, 0) * sign

    def close(i, carry):
        results = [finish(2 * i), finish(2 * i + 1)]
        for ref, n in ((plus_ref, 0), (minus_ref, 1)):
            both = jnp.concatenate([r[n] for r in results], axis=0)
            ref[pl.ds(4 * i, 4)] = both.reshape(4, 4, 128).astype(jnp.bfloat16)
        return carry

    lax.fori_loop(0, 32, close, 0, unroll=4)

    pltpu.make_async_copy(stage.at[0:3], stage.at[0:3], block_send).wait()

    pltpu.make_async_copy(trials.at[0:15], trials.at[0:15], trial_send).wait()

    @pl.when(jnp.logical_not(mine))
    def _():
        pltpu.make_async_copy(trials.at[0], trials.at[0], trial_send).wait()

    @pl.when(mine)
    def _():
        pltpu.make_async_copy(outgoing.at[0:15], outgoing.at[0:15], term_send).wait()
        pltpu.make_async_copy(outgoing.at[0, 0:7], outgoing.at[0, 0:7], term_send).wait()

    @pl.when(jnp.logical_not(mine))
    def _():
        pltpu.make_async_copy(outgoing, outgoing, term_send).wait()


def deliver(plus_ref, minus_ref, plus_out, minus_out, sems):
    copies = [
        pltpu.make_async_copy(plus_ref, plus_out, sems.at[0]),
        pltpu.make_async_copy(minus_ref, minus_out, sems.at[1]),
    ]
    for copy in copies:
        copy.start()
    for copy in copies:
        copy.wait()


def local(cholesky, trial_rows, occupied, kpoint_map, partner):
    blocks = cholesky.reshape(64, 2, 16, 128)
    trial = trial_rows.reshape(2, 32, 128)
    vmem = pl.BlockSpec(memory_space=pltpu.VMEM)
    bf16, i32 = jnp.bfloat16, jnp.int32
    plus, minus = pl.pallas_call(
        kernel,
        out_shape=[jax.ShapeDtypeStruct((128, 4, 128), bf16)] * 2,
        in_specs=[pl.BlockSpec(memory_space=pl.ANY)] * 5,
        out_specs=[vmem, vmem],
        scratch_shapes=[
            pltpu.VMEM((64, 2, 16, 128), bf16),
            pltpu.VMEM((2, 32, 128), bf16),
            pltpu.VMEM((2, 32, 128), bf16),
            pltpu.SMEM((64,), i32),
            pltpu.SMEM((64, 64), i32),
            pltpu.SMEM((64,), i32),
            pltpu.VMEM((4, 8, 2, 2, 2, 16, 128), bf16),
            pltpu.VMEM((8, 2, 2, 2, 128, 128), bf16),
            pltpu.VMEM((16, 2, 32, 128), bf16),
            pltpu.VMEM((16, 8, 7, 128), i32),
            pltpu.VMEM((2, 64, 7, 128), i32),
            pltpu.VMEM((64, 8, 128), jnp.float32),
            pltpu.VMEM((64, 8, 128), jnp.float32),
            pltpu.SemaphoreType.REGULAR,
            pltpu.SemaphoreType.DMA((5,)),
            pltpu.SemaphoreType.DMA,
            pltpu.SemaphoreType.DMA((8, 4)),
            pltpu.SemaphoreType.DMA,
            pltpu.SemaphoreType.DMA((16,)),
            pltpu.SemaphoreType.DMA,
            pltpu.SemaphoreType.DMA((8,)),
        ],
        compiler_params=pltpu.CompilerParams(
            collective_id=0, has_side_effects=True, vmem_limit_bytes=32 * 2**20
        ),
    )(*[pltpu.with_memory_space_constraint(a, pltpu.HBM) for a in (blocks, trial, occupied, kpoint_map, partner)])
    anywhere = pl.BlockSpec(memory_space=pltpu.HBM)
    plus, minus = pl.pallas_call(
        deliver,
        out_shape=[jax.ShapeDtypeStruct((128, 4, 128), bf16)] * 2,
        in_specs=[vmem, vmem],
        out_specs=[anywhere, anywhere],
        scratch_shapes=[pltpu.SemaphoreType.DMA((2,))],
        compiler_params=pltpu.CompilerParams(vmem_limit_bytes=32 * 2**20),
    )(plus, minus)
    shape = (1, 64, 1, 2, 4, 128)
    return plus.reshape(shape), minus.reshape(shape)


def solution(mesh):
    in_specs = (P("pb", None, None, None, "vert", None), P("pb", None, None, None), P(), P(), P())
    out_specs = (P("pb", None, None, None, "vert", None), P("pb", None, None, None, "vert", None))
    return jax.shard_map(local, mesh=mesh, in_specs=in_specs, out_specs=out_specs, check_vma=False)
```

```python
import functools

import jax
import jax.numpy as jnp
from jax import lax
from jax.experimental import pallas as pl
from jax.experimental.pallas import tpu as pltpu
from jax.sharding import PartitionSpec as P

MESH = pl.DeviceIdType.MESH
BITS = 17
TOP = 2**BITS - 1
BIAS = 128


def kpoint(jp, cp, y, zl):
    return jp * 8 + ((y - jp + zl + 8) % 4) * 2 + cp


def encode(own, real, imag):
    peak = jnp.maximum(jnp.maximum(jnp.abs(own), jnp.abs(real)), jnp.abs(imag))
    peak = jnp.max(peak, axis=0, keepdims=True)
    power = jnp.floor(jnp.log2(jnp.maximum(peak, 2.0**-100))) + 1.0
    scale = jnp.exp2(BITS - power)
    biased = (power.astype(jnp.int32) + BIAS) << 24
    row = lax.broadcasted_iota(jnp.int32, (8, 128), 0)
    low = row < 4
    place = (row % 4) * 6

    def code(value, t):
        return jnp.clip(jnp.round(value[8 * t : 8 * t + 8] * scale), -TOP, TOP).astype(jnp.int32)

    messages = []
    for t in range(4):
        a, b, c = code(real, t), code(imag, t), code(own, t)
        mirror = ((a >> 2) << 16) | ((b >> 2) & 65535)
        pairs = ((c >> 2) << 16) | pltpu.roll((c >> 2) & 65535, 6, 0)
        small = (((a & 3) << 4) | ((b & 3) << 2) | (c & 3)) << place
        small = small + pltpu.roll(small, 7, 0)
        small = (small + pltpu.roll(small, 6, 0)) | biased
        rest = jnp.where(row % 4 < 2, pairs, pltpu.roll(small, 2, 0))
        messages.append(jnp.where(low, mirror, pltpu.roll(rest, 4, 0)))
        messages.append(jnp.where(low, pltpu.roll(mirror, 4, 0), rest))
    return messages


def unit_of(word):
    return jnp.exp2((((word >> 24) & 255) - (BIAS + BITS)).astype(jnp.float32))


def kernel(
    blocks_hbm, trial_hbm, occupied_hbm, map_hbm, partner_hbm, plus_ref, minus_ref,
    blocks, trial_ref, masked, occupied, kpoint_map, partner, stage, work, trials, outgoing, incoming, relay, own_terms, mirror_terms,
    plane_in, relay_send, relay_recv, load_sem, block_send, block_recv, trial_send, trial_recv, term_send, term_recv,
):
    me, v = lax.axis_index("pb"), lax.axis_index("vert")
    zl, x, c = me // 8, (me // 2) % 4, me % 2
    zh, y = v // 4, v % 4
    z = zh * 8 + zl
    mine = x == y
    slot_me = 2 * zl + c
    offset = (y - x + 4) % 4
    first_zl = (zl + offset + 4 * (offset // 3)) % 8
    second_zl = (first_zl + 4) % 8

    loads = [
        pltpu.make_async_copy(a, b, load_sem.at[n])
        for n, (a, b) in enumerate(
            [(blocks_hbm, blocks), (trial_hbm, trial_ref), (occupied_hbm, occupied), (map_hbm, kpoint_map), (partner_hbm, partner)]
        )
    ]
    for load in loads:
        load.start()

    barrier = pltpu.get_barrier_semaphore()

    def greet(pb, vert):
        pl.semaphore_signal(barrier, inc=1, device_id=(pb, vert), device_id_type=MESH)

    def greet_ring(i, carry):
        there = (z + i) % 16
        greet((there % 8) * 8 + x * 2 + c, (there // 8) * 4 + y)
        return carry

    def greet_plane(i, carry):
        greet(zl * 8 + ((x + i // 8) % 4) * 2 + (c + i) % 2, zh * 4 + (y + i // 2) % 4)
        return carry

    for n, i in enumerate((8, 7, 9, 6, 10, 5, 11, 4, 12, 3, 13, 2, 14, 1, 15)):
        greet_ring(i, 0)
        greet_plane(2 * n + 1, 0)
        greet_plane(2 * n + 2, 0)
    greet_plane(31, 0)

    away = pl.multiple_of((1 - zh) * 64, 64)

    def clear(jp, carry):
        for cp in range(2):
            for part in range(2):
                work[jp, cp, 1, part, pl.ds(away, 64), :] = jnp.zeros((64, 128), jnp.bfloat16)
        return carry

    lax.fori_loop(0, 8, clear, 0)
    for load in loads:
        load.wait()

    live = lax.broadcasted_iota(jnp.int32, (32, 128), 0) < occupied[me]
    for part in range(2):
        value = trial_ref[part].astype(jnp.float32)
        masked[part] = jnp.where(live, value, 0.0).astype(jnp.bfloat16)

    @pl.when(mine)
    def _():
        trials[slot_me] = masked[...]

    mirror_q = partner[me]

    def arrange(jp, carry):
        for to in range(4):
            for cp in range(2):
                k = kpoint(jp, cp, to, zl)
                stage[to, jp, cp, 0, 0] = blocks[k, 0]
                stage[to, jp, cp, 0, 1] = -blocks[k, 1]
                stage[to, jp, cp, 1] = blocks[kpoint_map[mirror_q, k]]
        return carry

    lax.fori_loop(0, 8, arrange, 0)

    pl.semaphore_wait(barrier, 46)

    def tell_ring(i, carry):
        there = (z + i) % 16
        pl.semaphore_signal(
            plane_in, inc=1, device_id=((there % 8) * 8 + x * 2 + c, (there // 8) * 4 + y), device_id_type=MESH
        )
        return carry

    for i in (8, 7, 9, 6, 10, 5, 11, 4, 12, 3, 13, 2, 14, 1, 15):
        tell_ring(i, 0)

    def plane_at(i, sign=1):
        return (zl + sign * ((i + 1) // 2) * (2 * (i % 2) - 1) + 8) % 8

    def rows_from(jp, source):
        start = pl.multiple_of(zh * 64 + source * 16, 16)
        return work.at[jp, :, :, :, pl.ds(start, 16), :]

    def block_copy(i, d, source, target):
        jp = plane_at(i)
        return pltpu.make_async_remote_copy(
            src_ref=stage.at[target, jp],
            dst_ref=rows_from(jp, source),
            send_sem=block_send,
            recv_sem=block_recv.at[i, d],
            device_id=(me, zh * 4 + target),
            device_id_type=MESH,
        )

    def self_copy(i):
        jp = plane_at(i)
        return pltpu.make_async_copy(stage.at[y, jp], rows_from(jp, y), block_recv.at[i, 0])

    def trial_copy(slot, pb, vert, source=None):
        return pltpu.make_async_remote_copy(
            src_ref=trials.at[slot] if source is None else source,
            dst_ref=trials.at[slot],
            send_sem=trial_send,
            recv_sem=trial_recv.at[slot],
            device_id=(pb, vert),
            device_id_type=MESH,
        )

    def forward(there):
        for i in range(1, 8):
            trial_copy(2 * there + c, zl * 8 + ((x + i // 2) % 4) * 2 + (c + i) % 2, v).start()

    def block_sends(i, carry):
        self_copy(i).start()
        for d in range(1, 4):
            block_copy(i, d, y, (y + d) % 4).start()
        return carry

    block_sends(0, 0)

    def trial_along(d):
        there = (z - d + 16) % 16
        trial_copy(slot_me, (there % 8) * 8 + x * 2 + c, (there // 8) * 4 + y, masked).start()

    @pl.when(mine)
    def _():
        forward(zl)

    @pl.when(jnp.logical_not(mine))
    def _():
        trial_along(offset)

    trial_along(offset - 4)
    lax.fori_loop(1, 8, block_sends, 0, unroll=True)

    @pl.when(jnp.logical_not(mine))
    def _():
        trial_copy(2 * first_zl + c, me, v).wait_recv()
        forward(first_zl)


    here = pl.multiple_of(zh * 64, 64)
    low = lax.broadcasted_iota(jnp.int32, (8, 128), 0) < 4

    def send_term(source, k, w, sender_zh):
        own_tile = (k == me) & (w == v)
        target = incoming.at[sender_zh, me]

        @pl.when(own_tile)
        def _():
            pltpu.make_async_copy(source, target, term_recv.at[zl]).start()

        @pl.when(jnp.logical_not(own_tile))
        def _():
            pltpu.make_async_remote_copy(
                src_ref=source,
                dst_ref=target,
                send_sem=term_send,
                recv_sem=term_recv.at[zl],
                device_id=(k, w),
                device_id_type=MESH,
            ).start()

    def relay_copy(slot, cp):
        return pltpu.make_async_remote_copy(
            src_ref=outgoing.at[slot, pl.ds((1 - zh) * 4, 4)],
            dst_ref=relay.at[cp],
            send_sem=relay_send,
            recv_sem=relay_recv,
            device_id=(me, (1 - zh) * 4 + y),
            device_id_type=MESH,
        )

    def hand_on():
        pltpu.make_async_copy(relay, relay, relay_recv).wait()
        for cp in range(2):
            for n in range(4):
                send_term(relay.at[cp, n], kpoint(zl, cp, y, zl), zh * 4 + n, 1 - zh)

    def terms(first, i, carry):
        jp = plane_at(i)
        if not first:

            @pl.when(i == 2)
            def _():
                trial_copy(2 * second_zl + c, me, v).wait_recv()
                forward(second_zl)

            @pl.when(i == 4)
            def _():
                hand_on()

        self_copy(i).wait()
        for d in range(1, 4):
            block_copy(i, d, (y - d + 4) % 4, y).wait_recv()
        for cp in range(2):
            slot = 2 * jp + cp

            @pl.when((cp != c) | ((jp != first_zl) & (jp != second_zl)))
            def _():
                trial_copy(slot, me, v).wait_recv()

            real, imag = trials[slot, 0], trials[slot, 1]
            left = jnp.concatenate(
                [jnp.concatenate([real, imag], axis=1), jnp.concatenate([imag, -real], axis=1)], axis=0
            )
            mirror = jnp.dot(left, work[jp, cp, 1].reshape(256, 128), preferred_element_type=jnp.float32)
            right = jnp.concatenate(
                [work[jp, cp, 0, 0, pl.ds(here, 64), :], work[jp, cp, 0, 1, pl.ds(here, 64), :]], axis=1
            )
            own = lax.dot_general(
                left, right, (((1,), (1,)), ((), ())), preferred_element_type=jnp.float32
            )
            own = jnp.concatenate([own[:32], own[32:]], axis=1)
            messages = encode(own, mirror[:32], mirror[32:])
            k = kpoint(jp, cp, y, zl)
            for w in range(8):
                outgoing[slot, w] = messages[w][:7]
            if first:
                for n in range(4):
                    send_term(outgoing.at[slot, zh * 4 + n], k, zh * 4 + n, zh)
                relay_copy(slot, cp).start()
                continue
            if cp == 0:

                @pl.when(i == 1)
                def _():
                    pl.semaphore_wait(plane_in, 15)

            for w in range(8):
                send_term(outgoing.at[slot, w], k, w, zh)

        return carry

    terms(True, 0, 0)
    lax.fori_loop(1, 8, functools.partial(terms, False), 0)

    lane = lax.broadcasted_iota(jnp.int32, (8, 128), 1) < 64
    stay = low == lane
    sign = jnp.where(low, 0.5, -0.5)

    row = lax.broadcasted_iota(jnp.int32, (8, 128), 0)
    own_place = (row % 4) * 6
    mirror_place = own_place + jnp.where(low, 4, 2)

    def own_of(q):
        parts = []
        for h in range(2):
            pairs = incoming[h, q, pl.ds(4, 2)]
            parts += [pairs >> 16, (pairs << 16) >> 16]
        first, second = incoming[0, q, pl.ds(6, 1)], incoming[1, q, pl.ds(6, 1)]
        small = (jnp.where(low, first, second) >> own_place) & 3
        code = (jnp.concatenate(parts, axis=0) << 2) | small
        own = code.astype(jnp.float32) * jnp.where(low, unit_of(first), unit_of(second))
        return jnp.where(stay, own, pltpu.roll(pltpu.roll(own, 4, 0), 64, 1))

    def mirror_of(p, h):
        words, last = incoming[h, p, pl.ds(0, 4)], incoming[h, p, pl.ds(6, 1)]
        code = jnp.concatenate([words >> 16, (words << 16) >> 16], axis=0)
        code = (code << 2) | ((last >> mirror_place) & 3)
        return code.astype(jnp.float32) * unit_of(last)

    def decode(o, carry):
        plane = plane_at(o, -1)
        start = pl.multiple_of(plane * 8, 8)
        part = incoming.at[:, pl.ds(start, 8)]
        pltpu.make_async_copy(part, part, term_recv.at[plane]).wait()

        def one(n, carry):
            q = start + n
            own_terms[q] = own_of(q)
            mirror_terms[q] = mirror_of(q, 0) + mirror_of(q, 1)
            return carry

        return lax.fori_loop(0, 8, one, carry, unroll=4)

    lax.fori_loop(0, 8, decode, 0)

    def finish(q):
        own, mirror = own_terms[q], mirror_terms[partner[q]]
        return (own + mirror) * 0.5, pltpu.roll(own - mirror, 4, 0) * sign

    def close(i, carry):
        results = [finish(2 * i), finish(2 * i + 1)]
        for ref, n in ((plus_ref, 0), (minus_ref, 1)):
            both = jnp.concatenate([r[n] for r in results], axis=0)
            ref[pl.ds(4 * i, 4)] = both.reshape(4, 4, 128).astype(jnp.bfloat16)
        return carry

    lax.fori_loop(0, 32, close, 0, unroll=4)

    pltpu.make_async_copy(relay, relay, relay_send).wait()
    pltpu.make_async_copy(stage.at[0:3], stage.at[0:3], block_send).wait()

    pltpu.make_async_copy(trials.at[0:15], trials.at[0:15], trial_send).wait()

    @pl.when(jnp.logical_not(mine))
    def _():
        pltpu.make_async_copy(trials.at[0], trials.at[0], trial_send).wait()

    @pl.when(mine)
    def _():
        pltpu.make_async_copy(outgoing.at[0:15], outgoing.at[0:15], term_send).wait()
        pltpu.make_async_copy(outgoing.at[0, 0:6], outgoing.at[0, 0:6], term_send).wait()

    @pl.when(jnp.logical_not(mine))
    def _():
        pltpu.make_async_copy(outgoing, outgoing, term_send).wait()


def deliver(plus_ref, minus_ref, plus_out, minus_out, sems):
    copies = [
        pltpu.make_async_copy(plus_ref, plus_out, sems.at[0]),
        pltpu.make_async_copy(minus_ref, minus_out, sems.at[1]),
    ]
    for copy in copies:
        copy.start()
    for copy in copies:
        copy.wait()


def local(cholesky, trial_rows, occupied, kpoint_map, partner):
    blocks = cholesky.reshape(64, 2, 16, 128)
    trial = trial_rows.reshape(2, 32, 128)
    vmem = pl.BlockSpec(memory_space=pltpu.VMEM)
    bf16, i32 = jnp.bfloat16, jnp.int32
    plus, minus = pl.pallas_call(
        kernel,
        out_shape=[jax.ShapeDtypeStruct((128, 4, 128), bf16)] * 2,
        in_specs=[pl.BlockSpec(memory_space=pl.ANY)] * 5,
        out_specs=[vmem, vmem],
        scratch_shapes=[
            pltpu.VMEM((64, 2, 16, 128), bf16),
            pltpu.VMEM((2, 32, 128), bf16),
            pltpu.VMEM((2, 32, 128), bf16),
            pltpu.SMEM((64,), i32),
            pltpu.SMEM((64, 64), i32),
            pltpu.SMEM((64,), i32),
            pltpu.VMEM((4, 8, 2, 2, 2, 16, 128), bf16),
            pltpu.VMEM((8, 2, 2, 2, 128, 128), bf16),
            pltpu.VMEM((16, 2, 32, 128), bf16),
            pltpu.VMEM((16, 8, 7, 128), i32),
            pltpu.VMEM((2, 64, 7, 128), i32),
            pltpu.VMEM((2, 4, 7, 128), i32),
            pltpu.VMEM((64, 8, 128), jnp.float32),
            pltpu.VMEM((64, 8, 128), jnp.float32),
            pltpu.SemaphoreType.REGULAR,
            pltpu.SemaphoreType.DMA,
            pltpu.SemaphoreType.DMA,
            pltpu.SemaphoreType.DMA((5,)),
            pltpu.SemaphoreType.DMA,
            pltpu.SemaphoreType.DMA((8, 4)),
            pltpu.SemaphoreType.DMA,
            pltpu.SemaphoreType.DMA((16,)),
            pltpu.SemaphoreType.DMA,
            pltpu.SemaphoreType.DMA((8,)),
        ],
        compiler_params=pltpu.CompilerParams(
            collective_id=0, has_side_effects=True, vmem_limit_bytes=32 * 2**20
        ),
    )(*[pltpu.with_memory_space_constraint(a, pltpu.HBM) for a in (blocks, trial, occupied, kpoint_map, partner)])
    anywhere = pl.BlockSpec(memory_space=pltpu.HBM)
    plus, minus = pl.pallas_call(
        deliver,
        out_shape=[jax.ShapeDtypeStruct((128, 4, 128), bf16)] * 2,
        in_specs=[vmem, vmem],
        out_specs=[anywhere, anywhere],
        scratch_shapes=[pltpu.SemaphoreType.DMA((2,))],
        compiler_params=pltpu.CompilerParams(vmem_limit_bytes=32 * 2**20),
    )(plus, minus)
    shape = (1, 64, 1, 2, 4, 128)
    return plus.reshape(shape), minus.reshape(shape)


def solution(mesh):
    in_specs = (P("pb", None, None, None, "vert", None), P("pb", None, None, None), P(), P(), P())
    out_specs = (P("pb", None, None, None, "vert", None), P("pb", None, None, None, "vert", None))
    return jax.shard_map(local, mesh=mesh, in_specs=in_specs, out_specs=out_specs, check_vma=False)
```

```python
import functools

import jax
import jax.numpy as jnp
from jax import lax
from jax.experimental import pallas as pl
from jax.experimental.pallas import tpu as pltpu
from jax.sharding import PartitionSpec as P

MESH = pl.DeviceIdType.MESH
BITS = 17
TOP = 2**BITS - 1
BIAS = 128


def kpoint(jp, cp, y, zl):
    return jp * 8 + ((y - jp + zl + 8) % 4) * 2 + cp


def encode(own, real, imag):
    peak = jnp.maximum(jnp.maximum(jnp.abs(own), jnp.abs(real)), jnp.abs(imag))
    peak = jnp.max(peak, axis=0, keepdims=True)
    power = jnp.floor(jnp.log2(jnp.maximum(peak, 2.0**-100))) + 1.0
    scale = jnp.exp2(BITS - power)
    biased = (power.astype(jnp.int32) + BIAS) << 24
    row = lax.broadcasted_iota(jnp.int32, (8, 128), 0)
    low = row < 4
    place = (row % 4) * 6

    def code(value, t):
        return jnp.clip(jnp.round(value[8 * t : 8 * t + 8] * scale), -TOP, TOP).astype(jnp.int32)

    messages = []
    for t in range(4):
        a, b, c = code(real, t), code(imag, t), code(own, t)
        mirror = ((a >> 2) << 16) | ((b >> 2) & 65535)
        pairs = ((c >> 2) << 16) | pltpu.roll((c >> 2) & 65535, 6, 0)
        small = (((a & 3) << 4) | ((b & 3) << 2) | (c & 3)) << place
        small = small + pltpu.roll(small, 7, 0)
        small = (small + pltpu.roll(small, 6, 0)) | biased
        rest = jnp.where(row % 4 < 2, pairs, pltpu.roll(small, 2, 0))
        messages.append(jnp.where(low, mirror, pltpu.roll(rest, 4, 0)))
        messages.append(jnp.where(low, pltpu.roll(mirror, 4, 0), rest))
    return messages


def unit_of(word):
    return jnp.exp2((((word >> 24) & 255) - (BIAS + BITS)).astype(jnp.float32))


def kernel(
    blocks_hbm, trial_hbm, occupied_hbm, map_hbm, partner_hbm, plus_ref, minus_ref,
    blocks, trial_ref, masked, occupied, kpoint_map, partner, stage, work, trials, outgoing, incoming, relay, relayed, own_terms, mirror_terms,
    plane_in, relay_send, relay_recv, next_send, next_recv, load_sem, block_send, block_recv, trial_send, trial_recv, term_send, term_recv,
):
    me, v = lax.axis_index("pb"), lax.axis_index("vert")
    zl, x, c = me // 8, (me // 2) % 4, me % 2
    zh, y = v // 4, v % 4
    z = zh * 8 + zl
    mine = x == y
    slot_me = 2 * zl + c
    offset = (y - x + 4) % 4
    first_zl = (zl + offset + 4 * (offset // 3)) % 8
    second_zl = (first_zl + 4) % 8

    loads = [
        pltpu.make_async_copy(a, b, load_sem.at[n])
        for n, (a, b) in enumerate(
            [(blocks_hbm, blocks), (trial_hbm, trial_ref), (occupied_hbm, occupied), (map_hbm, kpoint_map), (partner_hbm, partner)]
        )
    ]
    for load in loads:
        load.start()

    barrier = pltpu.get_barrier_semaphore()

    def greet(pb, vert):
        pl.semaphore_signal(barrier, inc=1, device_id=(pb, vert), device_id_type=MESH)

    def greet_ring(i, carry):
        there = (z + i) % 16
        greet((there % 8) * 8 + x * 2 + c, (there // 8) * 4 + y)
        return carry

    def greet_plane(i, carry):
        greet(zl * 8 + ((x + i // 8) % 4) * 2 + (c + i) % 2, zh * 4 + (y + i // 2) % 4)
        return carry

    for n, i in enumerate((8, 7, 9, 6, 10, 5, 11, 4, 12, 3, 13, 2, 14, 1, 15)):
        greet_ring(i, 0)
        greet_plane(2 * n + 1, 0)
        greet_plane(2 * n + 2, 0)
    greet_plane(31, 0)

    away = pl.multiple_of((1 - zh) * 64, 64)

    def clear(jp, carry):
        for cp in range(2):
            for part in range(2):
                work[jp, cp, 1, part, pl.ds(away, 64), :] = jnp.zeros((64, 128), jnp.bfloat16)
        return carry

    lax.fori_loop(0, 8, clear, 0)
    for load in loads:
        load.wait()

    live = lax.broadcasted_iota(jnp.int32, (32, 128), 0) < occupied[me]
    for part in range(2):
        value = trial_ref[part].astype(jnp.float32)
        masked[part] = jnp.where(live, value, 0.0).astype(jnp.bfloat16)

    @pl.when(mine)
    def _():
        trials[slot_me] = masked[...]

    mirror_q = partner[me]

    def arrange(jp, carry):
        for to in range(4):
            for cp in range(2):
                k = kpoint(jp, cp, to, zl)
                stage[to, jp, cp, 0, 0] = blocks[k, 0]
                stage[to, jp, cp, 0, 1] = -blocks[k, 1]
                stage[to, jp, cp, 1] = blocks[kpoint_map[mirror_q, k]]
        return carry

    lax.fori_loop(0, 8, arrange, 0)

    pl.semaphore_wait(barrier, 46)

    def tell_ring(i, carry):
        there = (z + i) % 16
        pl.semaphore_signal(
            plane_in, inc=1, device_id=((there % 8) * 8 + x * 2 + c, (there // 8) * 4 + y), device_id_type=MESH
        )
        return carry

    for i in (8, 7, 9, 6, 10, 5, 11, 4, 12, 3, 13, 2, 14, 1, 15):
        tell_ring(i, 0)

    def plane_at(i, sign=1):
        return (zl + sign * ((i + 1) // 2) * (2 * (i % 2) - 1) + 8) % 8

    def rows_from(jp, source):
        start = pl.multiple_of(zh * 64 + source * 16, 16)
        return work.at[jp, :, :, :, pl.ds(start, 16), :]

    def block_copy(i, d, source, target):
        jp = plane_at(i)
        return pltpu.make_async_remote_copy(
            src_ref=stage.at[target, jp],
            dst_ref=rows_from(jp, source),
            send_sem=block_send,
            recv_sem=block_recv.at[i, d],
            device_id=(me, zh * 4 + target),
            device_id_type=MESH,
        )

    def self_copy(i):
        jp = plane_at(i)
        return pltpu.make_async_copy(stage.at[y, jp], rows_from(jp, y), block_recv.at[i, 0])

    def trial_copy(slot, pb, vert, source=None):
        return pltpu.make_async_remote_copy(
            src_ref=trials.at[slot] if source is None else source,
            dst_ref=trials.at[slot],
            send_sem=trial_send,
            recv_sem=trial_recv.at[slot],
            device_id=(pb, vert),
            device_id_type=MESH,
        )

    def forward(there):
        for i in range(1, 8):
            trial_copy(2 * there + c, zl * 8 + ((x + i // 2) % 4) * 2 + (c + i) % 2, v).start()

    def block_sends(i, carry):
        self_copy(i).start()
        for d in range(1, 4):
            block_copy(i, d, y, (y + d) % 4).start()
        return carry

    block_sends(0, 0)

    def trial_along(d):
        there = (z - d + 16) % 16
        trial_copy(slot_me, (there % 8) * 8 + x * 2 + c, (there // 8) * 4 + y, masked).start()

    @pl.when(mine)
    def _():
        forward(zl)

    @pl.when(jnp.logical_not(mine))
    def _():
        trial_along(offset)

    trial_along(offset - 4)
    lax.fori_loop(1, 8, block_sends, 0, unroll=True)

    @pl.when(jnp.logical_not(mine))
    def _():
        trial_copy(2 * first_zl + c, me, v).wait_recv()
        forward(first_zl)


    here = pl.multiple_of(zh * 64, 64)
    low = lax.broadcasted_iota(jnp.int32, (8, 128), 0) < 4

    def send_term(source, k, w, sender_zh, sender_zl):
        own_tile = (k == me) & (w == v)
        target = incoming.at[sender_zh, sender_zl * 8 + x * 2 + c]

        @pl.when(own_tile)
        def _():
            pltpu.make_async_copy(source, target, term_recv.at[sender_zl]).start()

        @pl.when(jnp.logical_not(own_tile))
        def _():
            pltpu.make_async_remote_copy(
                src_ref=source,
                dst_ref=target,
                send_sem=term_send,
                recv_sem=term_recv.at[sender_zl],
                device_id=(k, w),
                device_id_type=MESH,
            ).start()

    def relay_copy(slot, cp):
        return pltpu.make_async_remote_copy(
            src_ref=outgoing.at[slot, pl.ds((1 - zh) * 4, 4)],
            dst_ref=relay.at[cp],
            send_sem=relay_send,
            recv_sem=relay_recv,
            device_id=(me, (1 - zh) * 4 + y),
            device_id_type=MESH,
        )

    def hand_on():
        pltpu.make_async_copy(relay, relay, relay_recv).wait()
        for cp in range(2):
            for n in range(4):
                send_term(relay.at[cp, n], kpoint(zl, cp, y, zl), zh * 4 + n, 1 - zh, zl)

    def relay_next(slot, cp, half):
        return pltpu.make_async_remote_copy(
            src_ref=outgoing.at[slot, pl.ds(half * 4, 4)],
            dst_ref=relayed.at[zh, cp],
            send_sem=next_send,
            recv_sem=next_recv,
            device_id=((zl + 1) % 8 * 8 + x * 2 + c, half * 4 + y),
            device_id_type=MESH,
        )

    def hand_on_next():
        pltpu.make_async_copy(relayed, relayed, next_recv).wait()
        before = (zl + 7) % 8
        for h in range(2):
            for cp in range(2):
                for n in range(4):
                    send_term(relayed.at[h, cp, n], kpoint(zl, cp, y, before), zh * 4 + n, h, before)

    def terms(early, i, carry):
        jp = plane_at(i)
        if not early:

            @pl.when(i == 2)
            def _():
                trial_copy(2 * second_zl + c, me, v).wait_recv()
                forward(second_zl)

            @pl.when(i == 4)
            def _():
                hand_on()

            @pl.when(i == 5)
            def _():
                hand_on_next()

        self_copy(i).wait()
        for d in range(1, 4):
            block_copy(i, d, (y - d + 4) % 4, y).wait_recv()
        for cp in range(2):
            slot = 2 * jp + cp

            @pl.when((cp != c) | ((jp != first_zl) & (jp != second_zl)))
            def _():
                trial_copy(slot, me, v).wait_recv()

            real, imag = trials[slot, 0], trials[slot, 1]
            left = jnp.concatenate(
                [jnp.concatenate([real, imag], axis=1), jnp.concatenate([imag, -real], axis=1)], axis=0
            )
            mirror = jnp.dot(left, work[jp, cp, 1].reshape(256, 128), preferred_element_type=jnp.float32)
            right = jnp.concatenate(
                [work[jp, cp, 0, 0, pl.ds(here, 64), :], work[jp, cp, 0, 1, pl.ds(here, 64), :]], axis=1
            )
            own = lax.dot_general(
                left, right, (((1,), (1,)), ((), ())), preferred_element_type=jnp.float32
            )
            own = jnp.concatenate([own[:32], own[32:]], axis=1)
            messages = encode(own, mirror[:32], mirror[32:])
            k = kpoint(jp, cp, y, zl)
            for w in range(8):
                outgoing[slot, w] = messages[w][:7]
            if early and i == 1:
                for half in range(2):
                    relay_next(slot, cp, half).start()
                continue
            if early:
                for n in range(4):
                    send_term(outgoing.at[slot, zh * 4 + n], k, zh * 4 + n, zh, zl)
                relay_copy(slot, cp).start()
                continue
            if cp == 0:

                @pl.when(i == 2)
                def _():
                    pl.semaphore_wait(plane_in, 15)

            for w in range(8):
                send_term(outgoing.at[slot, w], k, w, zh, zl)

        return carry

    terms(True, 0, 0)
    terms(True, 1, 0)
    lax.fori_loop(2, 8, functools.partial(terms, False), 0)

    lane = lax.broadcasted_iota(jnp.int32, (8, 128), 1) < 64
    stay = low == lane
    sign = jnp.where(low, 0.5, -0.5)

    row = lax.broadcasted_iota(jnp.int32, (8, 128), 0)
    own_place = (row % 4) * 6
    mirror_place = own_place + jnp.where(low, 4, 2)

    def own_of(q):
        parts = []
        for h in range(2):
            pairs = incoming[h, q, pl.ds(4, 2)]
            parts += [pairs >> 16, (pairs << 16) >> 16]
        first, second = incoming[0, q, pl.ds(6, 1)], incoming[1, q, pl.ds(6, 1)]
        small = (jnp.where(low, first, second) >> own_place) & 3
        code = (jnp.concatenate(parts, axis=0) << 2) | small
        own = code.astype(jnp.float32) * jnp.where(low, unit_of(first), unit_of(second))
        return jnp.where(stay, own, pltpu.roll(pltpu.roll(own, 4, 0), 64, 1))

    def mirror_of(p, h):
        words, last = incoming[h, p, pl.ds(0, 4)], incoming[h, p, pl.ds(6, 1)]
        code = jnp.concatenate([words >> 16, (words << 16) >> 16], axis=0)
        code = (code << 2) | ((last >> mirror_place) & 3)
        return code.astype(jnp.float32) * unit_of(last)

    def decode(o, carry):
        plane = plane_at(o, -1)
        start = pl.multiple_of(plane * 8, 8)
        part = incoming.at[:, pl.ds(start, 8)]
        pltpu.make_async_copy(part, part, term_recv.at[plane]).wait()

        def one(n, carry):
            q = start + n
            own_terms[q] = own_of(q)
            mirror_terms[q] = mirror_of(q, 0) + mirror_of(q, 1)
            return carry

        return lax.fori_loop(0, 8, one, carry, unroll=4)

    lax.fori_loop(0, 8, decode, 0)

    def finish(q):
        own, mirror = own_terms[q], mirror_terms[partner[q]]
        return (own + mirror) * 0.5, pltpu.roll(own - mirror, 4, 0) * sign

    def close(i, carry):
        results = [finish(2 * i), finish(2 * i + 1)]
        for ref, n in ((plus_ref, 0), (minus_ref, 1)):
            both = jnp.concatenate([r[n] for r in results], axis=0)
            ref[pl.ds(4 * i, 4)] = both.reshape(4, 4, 128).astype(jnp.bfloat16)
        return carry

    lax.fori_loop(0, 32, close, 0, unroll=4)

    pltpu.make_async_copy(relay, relay, relay_send).wait()
    pltpu.make_async_copy(relayed, relayed, next_send).wait()
    pltpu.make_async_copy(stage.at[0:3], stage.at[0:3], block_send).wait()

    pltpu.make_async_copy(trials.at[0:15], trials.at[0:15], trial_send).wait()

    @pl.when(jnp.logical_not(mine))
    def _():
        pltpu.make_async_copy(trials.at[0], trials.at[0], trial_send).wait()

    @pl.when(offset < 2)
    def _():
        pltpu.make_async_copy(outgoing.at[0:15], outgoing.at[0:15], term_send).wait()
        pltpu.make_async_copy(outgoing.at[0, 0:6], outgoing.at[0, 0:6], term_send).wait()

    @pl.when(offset >= 2)
    def _():
        pltpu.make_async_copy(outgoing, outgoing, term_send).wait()


def deliver(plus_ref, minus_ref, plus_out, minus_out, sems):
    copies = [
        pltpu.make_async_copy(plus_ref, plus_out, sems.at[0]),
        pltpu.make_async_copy(minus_ref, minus_out, sems.at[1]),
    ]
    for copy in copies:
        copy.start()
    for copy in copies:
        copy.wait()


def local(cholesky, trial_rows, occupied, kpoint_map, partner):
    blocks = cholesky.reshape(64, 2, 16, 128)
    trial = trial_rows.reshape(2, 32, 128)
    vmem = pl.BlockSpec(memory_space=pltpu.VMEM)
    bf16, i32 = jnp.bfloat16, jnp.int32
    plus, minus = pl.pallas_call(
        kernel,
        out_shape=[jax.ShapeDtypeStruct((128, 4, 128), bf16)] * 2,
        in_specs=[pl.BlockSpec(memory_space=pl.ANY)] * 5,
        out_specs=[vmem, vmem],
        scratch_shapes=[
            pltpu.VMEM((64, 2, 16, 128), bf16),
            pltpu.VMEM((2, 32, 128), bf16),
            pltpu.VMEM((2, 32, 128), bf16),
            pltpu.SMEM((64,), i32),
            pltpu.SMEM((64, 64), i32),
            pltpu.SMEM((64,), i32),
            pltpu.VMEM((4, 8, 2, 2, 2, 16, 128), bf16),
            pltpu.VMEM((8, 2, 2, 2, 128, 128), bf16),
            pltpu.VMEM((16, 2, 32, 128), bf16),
            pltpu.VMEM((16, 8, 7, 128), i32),
            pltpu.VMEM((2, 64, 7, 128), i32),
            pltpu.VMEM((2, 4, 7, 128), i32),
            pltpu.VMEM((2, 2, 4, 7, 128), i32),
            pltpu.VMEM((64, 8, 128), jnp.float32),
            pltpu.VMEM((64, 8, 128), jnp.float32),
            pltpu.SemaphoreType.REGULAR,
            pltpu.SemaphoreType.DMA,
            pltpu.SemaphoreType.DMA,
            pltpu.SemaphoreType.DMA,
            pltpu.SemaphoreType.DMA,
            pltpu.SemaphoreType.DMA((5,)),
            pltpu.SemaphoreType.DMA,
            pltpu.SemaphoreType.DMA((8, 4)),
            pltpu.SemaphoreType.DMA,
            pltpu.SemaphoreType.DMA((16,)),
            pltpu.SemaphoreType.DMA,
            pltpu.SemaphoreType.DMA((8,)),
        ],
        compiler_params=pltpu.CompilerParams(
            collective_id=0, has_side_effects=True, vmem_limit_bytes=32 * 2**20
        ),
    )(*[pltpu.with_memory_space_constraint(a, pltpu.HBM) for a in (blocks, trial, occupied, kpoint_map, partner)])
    anywhere = pl.BlockSpec(memory_space=pltpu.HBM)
    plus, minus = pl.pallas_call(
        deliver,
        out_shape=[jax.ShapeDtypeStruct((128, 4, 128), bf16)] * 2,
        in_specs=[vmem, vmem],
        out_specs=[anywhere, anywhere],
        scratch_shapes=[pltpu.SemaphoreType.DMA((2,))],
        compiler_params=pltpu.CompilerParams(vmem_limit_bytes=32 * 2**20),
    )(plus, minus)
    shape = (1, 64, 1, 2, 4, 128)
    return plus.reshape(shape), minus.reshape(shape)


def solution(mesh):
    in_specs = (P("pb", None, None, None, "vert", None), P("pb", None, None, None), P(), P(), P())
    out_specs = (P("pb", None, None, None, "vert", None), P("pb", None, None, None, "vert", None))
    return jax.shard_map(local, mesh=mesh, in_specs=in_specs, out_specs=out_specs, check_vma=False)
```

```python
import functools

import jax
import jax.numpy as jnp
from jax import lax
from jax.experimental import pallas as pl
from jax.experimental.pallas import tpu as pltpu
from jax.sharding import PartitionSpec as P

MESH = pl.DeviceIdType.MESH
BITS = 17
TOP = 2**BITS - 1
BIAS = 128


def kpoint(jp, cp, y, zl):
    return jp * 8 + ((y - jp + zl + 8) % 4) * 2 + cp


def encode(own, real, imag):
    peak = jnp.maximum(jnp.maximum(jnp.abs(own), jnp.abs(real)), jnp.abs(imag))
    peak = jnp.max(peak, axis=0, keepdims=True)
    power = jnp.floor(jnp.log2(jnp.maximum(peak, 2.0**-100))) + 1.0
    scale = jnp.exp2(BITS - power)
    biased = (power.astype(jnp.int32) + BIAS) << 24
    row = lax.broadcasted_iota(jnp.int32, (8, 128), 0)
    low = row < 4
    place = (row % 4) * 6

    def code(value, t):
        return jnp.clip(jnp.round(value[8 * t : 8 * t + 8] * scale), -TOP, TOP).astype(jnp.int32)

    messages = []
    for t in range(4):
        a, b, c = code(real, t), code(imag, t), code(own, t)
        mirror = ((a >> 2) << 16) | ((b >> 2) & 65535)
        pairs = ((c >> 2) << 16) | pltpu.roll((c >> 2) & 65535, 6, 0)
        small = (((a & 3) << 4) | ((b & 3) << 2) | (c & 3)) << place
        small = small + pltpu.roll(small, 7, 0)
        small = (small + pltpu.roll(small, 6, 0)) | biased
        rest = jnp.where(row % 4 < 2, pairs, pltpu.roll(small, 2, 0))
        messages.append(jnp.where(low, mirror, pltpu.roll(rest, 4, 0)))
        messages.append(jnp.where(low, pltpu.roll(mirror, 4, 0), rest))
    return messages


def unit_of(word):
    return jnp.exp2((((word >> 24) & 255) - (BIAS + BITS)).astype(jnp.float32))


def kernel(
    blocks_hbm, trial_hbm, occupied_hbm, map_hbm, partner_hbm, plus_ref, minus_ref,
    blocks, trial_ref, masked, occupied, kpoint_map, partner, stage, work, trials, outgoing, incoming, relay, relayed, own_terms, mirror_terms,
    plane_in, relay_send, relay_recv, next_send, next_recv, load_sem, block_send, block_recv, trial_send, trial_recv, term_send, term_recv,
):
    me, v = lax.axis_index("pb"), lax.axis_index("vert")
    zl, x, c = me // 8, (me // 2) % 4, me % 2
    zh, y = v // 4, v % 4
    z = zh * 8 + zl
    mine = x == y
    slot_me = 2 * zl + c
    offset = (y - x + 4) % 4
    first_zl = (zl + offset + 4 * (offset // 3)) % 8
    second_zl = (first_zl + 4) % 8

    loads = [
        pltpu.make_async_copy(a, b, load_sem.at[n])
        for n, (a, b) in enumerate(
            [(blocks_hbm, blocks), (trial_hbm, trial_ref), (occupied_hbm, occupied), (map_hbm, kpoint_map), (partner_hbm, partner)]
        )
    ]
    for load in loads:
        load.start()

    barrier = pltpu.get_barrier_semaphore()

    def greet(pb, vert):
        pl.semaphore_signal(barrier, inc=1, device_id=(pb, vert), device_id_type=MESH)

    def greet_ring(i, carry):
        there = (z + i) % 16
        greet((there % 8) * 8 + x * 2 + c, (there // 8) * 4 + y)
        return carry

    def greet_plane(i, carry):
        greet(zl * 8 + ((x + i // 8) % 4) * 2 + (c + i) % 2, zh * 4 + (y + i // 2) % 4)
        return carry

    for n, i in enumerate((8, 7, 9, 6, 10, 5, 11, 4, 12, 3, 13, 2, 14, 1, 15)):
        greet_ring(i, 0)
        greet_plane(2 * n + 1, 0)
        greet_plane(2 * n + 2, 0)
    greet_plane(31, 0)

    away = pl.multiple_of((1 - zh) * 64, 64)

    def clear(jp, carry):
        for cp in range(2):
            for part in range(2):
                work[jp, cp, 1, part, pl.ds(away, 64), :] = jnp.zeros((64, 128), jnp.bfloat16)
        return carry

    lax.fori_loop(0, 8, clear, 0)
    for load in loads:
        load.wait()

    live = lax.broadcasted_iota(jnp.int32, (32, 128), 0) < occupied[me]
    for part in range(2):
        value = trial_ref[part].astype(jnp.float32)
        masked[part] = jnp.where(live, value, 0.0).astype(jnp.bfloat16)

    @pl.when(mine)
    def _():
        trials[slot_me] = masked[...]

    mirror_q = partner[me]

    def arrange(jp, carry):
        for to in range(4):
            for cp in range(2):
                k = kpoint(jp, cp, to, zl)
                stage[to, jp, cp, 0, 0] = blocks[k, 0]
                stage[to, jp, cp, 0, 1] = -blocks[k, 1]
                stage[to, jp, cp, 1] = blocks[kpoint_map[mirror_q, k]]
        return carry

    lax.fori_loop(0, 8, arrange, 0)

    pl.semaphore_wait(barrier, 46)

    def plane_at(i, sign=1):
        return (zl + sign * ((i + 1) // 2) * (2 * (i % 2) - 1) + 8) % 8

    def rows_from(jp, source):
        start = pl.multiple_of(zh * 64 + source * 16, 16)
        return work.at[jp, :, :, :, pl.ds(start, 16), :]

    def block_copy(i, d, source, target):
        jp = plane_at(i)
        return pltpu.make_async_remote_copy(
            src_ref=stage.at[target, jp],
            dst_ref=rows_from(jp, source),
            send_sem=block_send,
            recv_sem=block_recv.at[i, d],
            device_id=(me, zh * 4 + target),
            device_id_type=MESH,
        )

    def self_copy(i):
        jp = plane_at(i)
        return pltpu.make_async_copy(stage.at[y, jp], rows_from(jp, y), block_recv.at[i, 0])

    def trial_copy(slot, pb, vert, source=None):
        return pltpu.make_async_remote_copy(
            src_ref=trials.at[slot] if source is None else source,
            dst_ref=trials.at[slot],
            send_sem=trial_send,
            recv_sem=trial_recv.at[slot],
            device_id=(pb, vert),
            device_id_type=MESH,
        )

    def forward(there):
        for i in range(1, 8):
            trial_copy(2 * there + c, zl * 8 + ((x + i // 2) % 4) * 2 + (c + i) % 2, v).start()

    def block_sends(i, carry):
        self_copy(i).start()
        for d in range(1, 4):
            block_copy(i, d, y, (y + d) % 4).start()
        return carry

    def trial_along(d):
        there = (z - d + 16) % 16
        trial_copy(slot_me, (there % 8) * 8 + x * 2 + c, (there // 8) * 4 + y, masked).start()

    @pl.when(mine)
    def _():
        forward(zl)

    @pl.when(jnp.logical_not(mine))
    def _():
        trial_along(offset)

    trial_along(offset - 4)
    def tell_ring(i, carry):
        there = (z + i) % 16
        pl.semaphore_signal(
            plane_in, inc=1, device_id=((there % 8) * 8 + x * 2 + c, (there // 8) * 4 + y), device_id_type=MESH
        )
        return carry

    for i in (8, 7, 9, 6, 10, 5, 11, 4, 12, 3, 13, 2, 14, 1, 15):
        tell_ring(i, 0)

    block_sends(0, 0)

    lax.fori_loop(1, 8, block_sends, 0, unroll=True)

    @pl.when(jnp.logical_not(mine))
    def _():
        trial_copy(2 * first_zl + c, me, v).wait_recv()
        forward(first_zl)


    here = pl.multiple_of(zh * 64, 64)
    low = lax.broadcasted_iota(jnp.int32, (8, 128), 0) < 4

    def send_term(source, k, w, sender_zh, sender_zl):
        own_tile = (k == me) & (w == v)
        target = incoming.at[sender_zh, sender_zl * 8 + x * 2 + c]

        @pl.when(own_tile)
        def _():
            pltpu.make_async_copy(source, target, term_recv.at[sender_zl]).start()

        @pl.when(jnp.logical_not(own_tile))
        def _():
            pltpu.make_async_remote_copy(
                src_ref=source,
                dst_ref=target,
                send_sem=term_send,
                recv_sem=term_recv.at[sender_zl],
                device_id=(k, w),
                device_id_type=MESH,
            ).start()

    def relay_copy(slot, cp):
        return pltpu.make_async_remote_copy(
            src_ref=outgoing.at[slot, pl.ds((1 - zh) * 4, 4)],
            dst_ref=relay.at[cp],
            send_sem=relay_send,
            recv_sem=relay_recv,
            device_id=(me, (1 - zh) * 4 + y),
            device_id_type=MESH,
        )

    def hand_on():
        pltpu.make_async_copy(relay, relay, relay_recv).wait()
        for cp in range(2):
            for n in range(4):
                send_term(relay.at[cp, n], kpoint(zl, cp, y, zl), zh * 4 + n, 1 - zh, zl)

    def relay_next(slot, cp, half):
        return pltpu.make_async_remote_copy(
            src_ref=outgoing.at[slot, pl.ds(half * 4, 4)],
            dst_ref=relayed.at[zh, cp],
            send_sem=next_send,
            recv_sem=next_recv,
            device_id=((zl + 1) % 8 * 8 + x * 2 + c, half * 4 + y),
            device_id_type=MESH,
        )

    def hand_on_next():
        pltpu.make_async_copy(relayed, relayed, next_recv).wait()
        before = (zl + 7) % 8
        for h in range(2):
            for cp in range(2):
                for n in range(4):
                    send_term(relayed.at[h, cp, n], kpoint(zl, cp, y, before), zh * 4 + n, h, before)

    def terms(early, i, carry):
        jp = plane_at(i)
        if not early:

            @pl.when(i == 2)
            def _():
                trial_copy(2 * second_zl + c, me, v).wait_recv()
                forward(second_zl)

            @pl.when(i == 4)
            def _():
                hand_on()

            @pl.when(i == 5)
            def _():
                hand_on_next()

        self_copy(i).wait()
        for d in range(1, 4):
            block_copy(i, d, (y - d + 4) % 4, y).wait_recv()
        for cp in range(2):
            slot = 2 * jp + cp

            @pl.when((cp != c) | ((jp != first_zl) & (jp != second_zl)))
            def _():
                trial_copy(slot, me, v).wait_recv()

            real, imag = trials[slot, 0], trials[slot, 1]
            left = jnp.concatenate(
                [jnp.concatenate([real, imag], axis=1), jnp.concatenate([imag, -real], axis=1)], axis=0
            )
            mirror = jnp.dot(left, work[jp, cp, 1].reshape(256, 128), preferred_element_type=jnp.float32)
            right = jnp.concatenate(
                [work[jp, cp, 0, 0, pl.ds(here, 64), :], work[jp, cp, 0, 1, pl.ds(here, 64), :]], axis=1
            )
            own = lax.dot_general(
                left, right, (((1,), (1,)), ((), ())), preferred_element_type=jnp.float32
            )
            own = jnp.concatenate([own[:32], own[32:]], axis=1)
            messages = encode(own, mirror[:32], mirror[32:])
            k = kpoint(jp, cp, y, zl)
            for w in range(8):
                outgoing[slot, w] = messages[w][:7]
            if early and i == 1:
                for half in range(2):
                    relay_next(slot, cp, half).start()
                continue
            if early:
                for n in range(4):
                    send_term(outgoing.at[slot, zh * 4 + n], k, zh * 4 + n, zh, zl)
                relay_copy(slot, cp).start()
                continue
            if cp == 0:

                @pl.when(i == 2)
                def _():
                    pl.semaphore_wait(plane_in, 15)

            for w in range(8):
                send_term(outgoing.at[slot, w], k, w, zh, zl)

        return carry

    terms(True, 0, 0)
    terms(True, 1, 0)
    lax.fori_loop(2, 8, functools.partial(terms, False), 0)

    lane = lax.broadcasted_iota(jnp.int32, (8, 128), 1) < 64
    stay = low == lane
    sign = jnp.where(low, 0.5, -0.5)

    row = lax.broadcasted_iota(jnp.int32, (8, 128), 0)
    own_place = (row % 4) * 6
    mirror_place = own_place + jnp.where(low, 4, 2)

    def own_of(q):
        parts = []
        for h in range(2):
            pairs = incoming[h, q, pl.ds(4, 2)]
            parts += [pairs >> 16, (pairs << 16) >> 16]
        first, second = incoming[0, q, pl.ds(6, 1)], incoming[1, q, pl.ds(6, 1)]
        small = (jnp.where(low, first, second) >> own_place) & 3
        code = (jnp.concatenate(parts, axis=0) << 2) | small
        own = code.astype(jnp.float32) * jnp.where(low, unit_of(first), unit_of(second))
        return jnp.where(stay, own, pltpu.roll(pltpu.roll(own, 4, 0), 64, 1))

    def mirror_of(p, h):
        words, last = incoming[h, p, pl.ds(0, 4)], incoming[h, p, pl.ds(6, 1)]
        code = jnp.concatenate([words >> 16, (words << 16) >> 16], axis=0)
        code = (code << 2) | ((last >> mirror_place) & 3)
        return code.astype(jnp.float32) * unit_of(last)

    def decode(o, carry):
        plane = plane_at(o, -1)
        start = pl.multiple_of(plane * 8, 8)
        part = incoming.at[:, pl.ds(start, 8)]
        pltpu.make_async_copy(part, part, term_recv.at[plane]).wait()

        def one(n, carry):
            q = start + n
            own_terms[q] = own_of(q)
            mirror_terms[q] = mirror_of(q, 0) + mirror_of(q, 1)
            return carry

        return lax.fori_loop(0, 8, one, carry, unroll=4)

    lax.fori_loop(0, 8, decode, 0)

    def finish(q):
        own, mirror = own_terms[q], mirror_terms[partner[q]]
        return (own + mirror) * 0.5, pltpu.roll(own - mirror, 4, 0) * sign

    def close(i, carry):
        results = [finish(2 * i), finish(2 * i + 1)]
        for ref, n in ((plus_ref, 0), (minus_ref, 1)):
            both = jnp.concatenate([r[n] for r in results], axis=0)
            ref[pl.ds(4 * i, 4)] = both.reshape(4, 4, 128).astype(jnp.bfloat16)
        return carry

    lax.fori_loop(0, 32, close, 0, unroll=4)

    pltpu.make_async_copy(relay, relay, relay_send).wait()
    pltpu.make_async_copy(relayed, relayed, next_send).wait()
    pltpu.make_async_copy(stage.at[0:3], stage.at[0:3], block_send).wait()

    pltpu.make_async_copy(trials.at[0:15], trials.at[0:15], trial_send).wait()

    @pl.when(jnp.logical_not(mine))
    def _():
        pltpu.make_async_copy(trials.at[0], trials.at[0], trial_send).wait()

    @pl.when(offset < 2)
    def _():
        pltpu.make_async_copy(outgoing.at[0:15], outgoing.at[0:15], term_send).wait()
        pltpu.make_async_copy(outgoing.at[0, 0:6], outgoing.at[0, 0:6], term_send).wait()

    @pl.when(offset >= 2)
    def _():
        pltpu.make_async_copy(outgoing, outgoing, term_send).wait()


def deliver(plus_ref, minus_ref, plus_out, minus_out, sems):
    copies = [
        pltpu.make_async_copy(plus_ref, plus_out, sems.at[0]),
        pltpu.make_async_copy(minus_ref, minus_out, sems.at[1]),
    ]
    for copy in copies:
        copy.start()
    for copy in copies:
        copy.wait()


def local(cholesky, trial_rows, occupied, kpoint_map, partner):
    blocks = cholesky.reshape(64, 2, 16, 128)
    trial = trial_rows.reshape(2, 32, 128)
    vmem = pl.BlockSpec(memory_space=pltpu.VMEM)
    bf16, i32 = jnp.bfloat16, jnp.int32
    plus, minus = pl.pallas_call(
        kernel,
        out_shape=[jax.ShapeDtypeStruct((128, 4, 128), bf16)] * 2,
        in_specs=[pl.BlockSpec(memory_space=pl.ANY)] * 5,
        out_specs=[vmem, vmem],
        scratch_shapes=[
            pltpu.VMEM((64, 2, 16, 128), bf16),
            pltpu.VMEM((2, 32, 128), bf16),
            pltpu.VMEM((2, 32, 128), bf16),
            pltpu.SMEM((64,), i32),
            pltpu.SMEM((64, 64), i32),
            pltpu.SMEM((64,), i32),
            pltpu.VMEM((4, 8, 2, 2, 2, 16, 128), bf16),
            pltpu.VMEM((8, 2, 2, 2, 128, 128), bf16),
            pltpu.VMEM((16, 2, 32, 128), bf16),
            pltpu.VMEM((16, 8, 7, 128), i32),
            pltpu.VMEM((2, 64, 7, 128), i32),
            pltpu.VMEM((2, 4, 7, 128), i32),
            pltpu.VMEM((2, 2, 4, 7, 128), i32),
            pltpu.VMEM((64, 8, 128), jnp.float32),
            pltpu.VMEM((64, 8, 128), jnp.float32),
            pltpu.SemaphoreType.REGULAR,
            pltpu.SemaphoreType.DMA,
            pltpu.SemaphoreType.DMA,
            pltpu.SemaphoreType.DMA,
            pltpu.SemaphoreType.DMA,
            pltpu.SemaphoreType.DMA((5,)),
            pltpu.SemaphoreType.DMA,
            pltpu.SemaphoreType.DMA((8, 4)),
            pltpu.SemaphoreType.DMA,
            pltpu.SemaphoreType.DMA((16,)),
            pltpu.SemaphoreType.DMA,
            pltpu.SemaphoreType.DMA((8,)),
        ],
        compiler_params=pltpu.CompilerParams(
            collective_id=0, has_side_effects=True, vmem_limit_bytes=32 * 2**20
        ),
    )(*[pltpu.with_memory_space_constraint(a, pltpu.HBM) for a in (blocks, trial, occupied, kpoint_map, partner)])
    anywhere = pl.BlockSpec(memory_space=pltpu.HBM)
    plus, minus = pl.pallas_call(
        deliver,
        out_shape=[jax.ShapeDtypeStruct((128, 4, 128), bf16)] * 2,
        in_specs=[vmem, vmem],
        out_specs=[anywhere, anywhere],
        scratch_shapes=[pltpu.SemaphoreType.DMA((2,))],
        compiler_params=pltpu.CompilerParams(vmem_limit_bytes=32 * 2**20),
    )(plus, minus)
    shape = (1, 64, 1, 2, 4, 128)
    return plus.reshape(shape), minus.reshape(shape)


def solution(mesh):
    in_specs = (P("pb", None, None, None, "vert", None), P("pb", None, None, None), P(), P(), P())
    out_specs = (P("pb", None, None, None, "vert", None), P("pb", None, None, None, "vert", None))
    return jax.shard_map(local, mesh=mesh, in_specs=in_specs, out_specs=out_specs, check_vma=False)
```
